32 devices in a mesh: dp: 16 (over z, y, core), tensor: 2 (over x).
Axes of the slice: x: 2, y: 2, z: 4, core: 2. Of those that a mesh axis runs over, the one named last changes fastest.
Arguments:
- inputs: bfloat16 [2, 16, 1024, 768], P(None, 'dp', 'tensor'), may hold values from -6 to 6
- cotangent: bfloat16 [2, 16, 1024, 768], P(None, 'dp', 'tensor'), may hold values from -6 to 6
- lengths: int32 [2, 16], P(None, 'dp'), may hold values from 64 to 1024, as said below
- gain_one: float32 [768], replicated, may hold values from 0.25 to 1.75
- shift_one: float32 [768], replicated, may hold values from -1.75 to 1.75
- qkv_weight: bfloat16 [768, 3, 768], P(None, None, 'tensor'), may hold values from -0.3125 to 0.3125
- qv_bias: float32 [2, 768], P(None, 'tensor'), may hold values from -1.75 to 1.75
- proj_weight: bfloat16 [768, 768], P('tensor'), may hold values from -6 to 6
- proj_bias: float32 [768], replicated, may hold values from -8 to 8
- gain_two: float32 [768], replicated, may hold values from 0.25 to 1.75
- shift_two: float32 [768], replicated, may hold values from -1.75 to 1.75
- fc_weight: bfloat16 [768, 3072], P(None, 'tensor'), may hold values from -0.21875 to 0.21875
- fc_bias: float32 [3072], P('tensor'), may hold values from -1.75 to 1.75
- out_weight: bfloat16 [3072, 768], P('tensor'), may hold values from -0.75 to 0.75
- out_bias: float32 [768], replicated, may hold values from -8 to 8
Outputs:
- outputs: float32 [2, 16, 1024, 768], P(None, 'dp', 'tensor')
- grad_inputs: float32 [2, 16, 1024, 768], P(None, 'dp', 'tensor')
- grad_gain_one: float32 [768], replicated
- grad_shift_one: float32 [768], replicated
- grad_qkv_weight: float32 [768, 3, 768], P(None, None, 'tensor')
- grad_qv_bias: float32 [2, 768], P(None, 'tensor')
- grad_proj_weight: float32 [768, 768], P('tensor')
- grad_proj_bias: float32 [768], replicated
- grad_gain_two: float32 [768], replicated
- grad_shift_two: float32 [768], replicated
- grad_fc_weight: float32 [768, 3072], P(None, 'tensor')
- grad_fc_bias: float32 [3072], P('tensor')
- grad_out_weight: float32 [3072, 768], P('tensor')
- grad_out_bias: float32 [768], replicated
The draws below stay inside these ranges and needn't reach their ends.
Inputs may be any that keep to these rules, and one draw needn't show every extreme that they name: `lengths`: in every micro-batch one sequence has length exactly 1024; short sequences are rare.
All inputs are finite; a program needn't handle non-finite values.
Results may differ from the reference program's by a relative error of at most 0.014.
Values may be sent and summed in bfloat16 or wider, within the bound.
A program may use at most 256 MiB of HBM per device.

```python
import jax
import jax.numpy as jnp
from jax import lax

D = 768
HEADS = 12
HEAD_DIM = 64
FF = 3072
LEN = 1024
MIN_LEN = 64
MICRO = 2
SEQS = 16


def draw_lengths(key, part):
    key = jax.random.fold_in(key, 7)
    key_one, key_two, key_three = jax.random.split(key, 3)
    span = LEN - MIN_LEN + 1
    first = jax.random.randint(key_one, (MICRO, SEQS), 0, span)
    second = jax.random.randint(key_two, (MICRO, SEQS), 0, span)
    shortfall = first * second // span
    drawn = MIN_LEN + (span - 1) - shortfall
    longest = jax.random.randint(key_three, (MICRO,), 0, SEQS)
    chosen = jnp.arange(SEQS, dtype=jnp.int32)[None, :] == longest[:, None]
    return jnp.where(chosen, LEN, drawn).astype(jnp.int32)


def shard_levels(stream_key, extent, pieces, smallest, top_value):
    def one(axis_at, parts):
        draws = jax.random.uniform(jax.random.fold_in(jax.random.fold_in(stream_key, 6), axis_at), (parts,), jnp.float32, smallest / len(pieces), top_value / len(pieces))
        return jnp.repeat(jnp.exp(draws), extent[axis_at] // parts).reshape((-1,) + (1,) * (len(extent) - axis_at - 1))

    factor_of = one(*pieces[0])
    for cut in pieces[1:]:
        factor_of = factor_of * one(*cut)
    return factor_of


def gaussian(rng, extent, deviation, most, shards=(), kind=jnp.bfloat16):
    values = deviation * jax.random.normal(rng, extent, jnp.float32)
    if shards:
        values = values * shard_levels(rng, extent, shards, -0.22, 0.18)
    return jnp.clip(values, -most, most).astype(kind)


def setup_inputs(seed: int = 0) -> dict:
    arg_keys = jax.random.split(jax.random.key(seed), 16)
    return {
        "inputs": gaussian(arg_keys[0], (MICRO, SEQS, LEN, D), 1.0, 6.0, ((1, 16), (2, 2))),
        "cotangent": gaussian(arg_keys[1], (MICRO, SEQS, LEN, D), 1.0, 6.0, ((1, 16), (2, 2))),
        "lengths": draw_lengths(jax.random.fold_in(arg_keys[15], 71), 0),
        "gain_one": jnp.clip(1.0 + 0.15 * jax.random.normal(arg_keys[3], (D,), jnp.float32), 0.25, 1.75),
        "shift_one": gaussian(arg_keys[4], (D,), 0.3, 1.75, (), jnp.float32),
        "qkv_weight": gaussian(arg_keys[5], (D, 3, D), (D // 2) ** -0.5, 0.3125, ((2, 2),)),
        "qv_bias": gaussian(arg_keys[6], (2, D), 0.3, 1.75, ((1, 2),), jnp.float32),
        "proj_weight": gaussian(arg_keys[7], (D, D), 1 ** -0.5, 6.0, ((0, 2),)),
        "proj_bias": gaussian(arg_keys[8], (D,), 1.5, 8.0, (), jnp.float32),
        "gain_two": jnp.clip(1.0 + 0.15 * jax.random.normal(arg_keys[9], (D,), jnp.float32), 0.25, 1.75),
        "shift_two": gaussian(arg_keys[10], (D,), 0.3, 1.75, (), jnp.float32),
        "fc_weight": gaussian(arg_keys[11], (D, FF), D ** -0.5, 0.21875, ((1, 2),)),
        "fc_bias": gaussian(arg_keys[12], (FF,), 0.3, 1.75, ((0, 2),), jnp.float32),
        "out_weight": gaussian(arg_keys[13], (FF, D), (FF // 48) ** -0.5, 0.75, ((0, 2),)),
        "out_bias": gaussian(arg_keys[14], (D,), 1.5, 8.0, (), jnp.float32),
    }


norm_eps = 1e-05
branch_scale = 48 ** (-0.5)
masked_value = -1e+30
highest_precision = lax.Precision.HIGHEST

@jax.custom_vjp
def low(v):
    return lax.optimization_barrier(v.astype(jnp.bfloat16)).astype(jnp.float32)

@jax.custom_vjp
def low_back(v):
    return v

def low_keep(v):
    return (low(v), None)

def low_pass(kept, grad):
    return (grad,)

def back_keep(v):
    return (v, None)

def back_low(kept, grad):
    return (low(grad),)
low.defvjp(low_keep, low_pass)
low_back.defvjp(back_keep, back_low)

def layer_norm(rows, gain, shift):
    centered = rows - lax.optimization_barrier(jnp.mean(rows, axis=-1, keepdims=True))
    variance = lax.optimization_barrier(jnp.mean(centered * centered, axis=-1, keepdims=True))
    return centered * lax.rsqrt(variance + norm_eps) * gain + shift

def attend(queries, keys, values, first_row, seq_length):
    query_ids = first_row + jnp.arange(queries.shape[0], dtype=jnp.int32)
    key_ids = jnp.arange(keys.shape[0], dtype=jnp.int32)
    allowed = (key_ids[None, :] <= query_ids[:, None]) & (key_ids[None, :] < seq_length)
    scores = jnp.einsum('qhe,khe->hqk', queries, keys, precision=highest_precision) * HEAD_DIM ** (-0.5)
    scores = jnp.where(allowed[None], low_back(scores), masked_value)
    row_max = lax.optimization_barrier(jnp.max(scores, axis=-1, keepdims=True))
    expd = jnp.exp(scores - row_max)
    weights = low(expd / lax.optimization_barrier(jnp.sum(expd, axis=-1, keepdims=True)))
    return jnp.einsum('hqk,khe->qhe', weights, values, precision=highest_precision)

def forward(seq_rows, seq_length, params):
    gain_one, shift_one, qkv_weight, qv_bias, proj_weight, proj_bias, gain_two, shift_two, fc_weight, fc_bias, out_weight, out_bias = params
    seq_len = seq_rows.shape[0]
    model_width = seq_rows.shape[1]
    normed = low(layer_norm(seq_rows, gain_one, shift_one))
    bias_flat = jnp.concatenate([qv_bias[0], jnp.zeros_like(qv_bias[0]), qv_bias[1]])
    projected = jnp.dot(normed, qkv_weight.reshape(model_width, 3 * model_width), precision=highest_precision) + bias_flat
    projected = low(low_back(projected)).reshape(seq_len, 3, HEADS, HEAD_DIM)
    queries = projected[:, 0]
    keys = projected[:, 1]
    values = projected[:, 2]
    block_rows = min(512, seq_len)
    block_count = seq_len // block_rows
    query_blocks = queries.reshape(block_count, block_rows, HEADS, HEAD_DIM)
    first_rows = jnp.arange(block_count, dtype=jnp.int32) * block_rows
    attend_step = jax.checkpoint(lambda item: attend(item[0], keys, values, item[1], seq_length))
    attended = lax.map(attend_step, (query_blocks, first_rows)).reshape(seq_len, model_width)
    mixed = low(low_back(attended))
    branch_attn = low_back(jnp.dot(mixed, proj_weight, precision=highest_precision))
    resid = seq_rows + branch_scale * (branch_attn + proj_bias)
    normed_two = low(layer_norm(resid, gain_two, shift_two))
    hidden_pre = low_back(jnp.dot(normed_two, fc_weight, precision=highest_precision) + fc_bias)
    hidden = low(jax.nn.gelu(hidden_pre, approximate=True))
    branch_mlp = low_back(jnp.dot(hidden, out_weight, precision=highest_precision))
    return resid + branch_scale * (branch_mlp + out_bias)

def reference(inputs, cotangent, lengths, gain_one, shift_one, qkv_weight, qv_bias, proj_weight, proj_bias, gain_two, shift_two, fc_weight, fc_bias, out_weight, out_bias):
    params = tuple((entry.astype(jnp.float32) for entry in (gain_one, shift_one, qkv_weight, qv_bias, proj_weight, proj_bias, gain_two, shift_two, fc_weight, fc_bias, out_weight, out_bias)))
    seq_inputs = inputs.astype(jnp.float32).reshape(-1, LEN, D)
    seq_cots = cotangent.astype(jnp.float32).reshape(-1, LEN, D)
    seq_lengths = lengths.reshape(-1)
    zero_grads = jax.tree.map(jnp.zeros_like, params)

    def one_sequence(carry, item):
        seq_rows, seq_cot, seq_length = item
        result, pullback = jax.vjp(lambda rows, weights: forward(rows, seq_length, weights), seq_rows, params)
        valid = (jnp.arange(LEN, dtype=jnp.int32) < seq_length).astype(jnp.float32)
        grad_rows, grad_params = pullback(seq_cot * valid[:, None])
        return (jax.tree.map(jnp.add, carry, grad_params), (result, grad_rows))
    totals, stacked = lax.scan(one_sequence, zero_grads, (seq_inputs, seq_cots, seq_lengths))
    grad_gain_one, grad_shift_one, grad_qkv, grad_qv, grad_proj, grad_proj_bias, grad_gain_two, grad_shift_two, grad_fc, grad_fc_bias, grad_out, grad_out_bias = totals
    outputs = stacked[0].reshape(inputs.shape)
    grad_inputs = stacked[1].reshape(inputs.shape)
    return (outputs, grad_inputs, grad_gain_one, grad_shift_one, grad_qkv, grad_qv, grad_proj, grad_proj_bias, grad_gain_two, grad_shift_two, grad_fc, grad_fc_bias, grad_out, grad_out_bias)
```

```python
import functools

import jax
import jax.numpy as jnp
from jax import lax
from jax.experimental import pallas as pl
from jax.experimental.pallas import tpu as pltpu
from jax.sharding import PartitionSpec as P

F = jnp.float32
B = jnp.bfloat16
T = 1024
D = 768
HD = 64
HW = 384
FF = 3072
FH = 1536
CH = 512
RT = 256
QB = 256
NP = 6
EPS = 1e-05
SB = 48 ** (-0.5)
RC = 0.7978845608028654
CC = 0.044715


def nn(a, b):
    return lax.dot_general(a, b, (((1,), (0,)), ((), ())), preferred_element_type=F)


def nt(a, b):
    return lax.dot_general(a, b, (((1,), (1,)), ((), ())), preferred_element_type=F)


def tn(a, b):
    return lax.dot_general(a, b, (((0,), (0,)), ((), ())), preferred_element_type=F)


def rows_of(r):
    return pl.ds(pl.multiple_of(r * RT, RT), RT)


def norm(v):
    cen = v - jnp.mean(v, axis=-1, keepdims=True)
    inv = lax.rsqrt(jnp.mean(cen * cen, axis=-1, keepdims=True) + EPS)
    return cen * inv, inv


def norm_back(e, n, inv):
    return inv * (e - jnp.mean(e, axis=-1, keepdims=True) - n * jnp.mean(e * n, axis=-1, keepdims=True))


def gelu_pair(u):
    u2 = u * u
    t = jnp.tanh(RC * (u + CC * u2 * u))
    hp = 0.5 * (1.0 + t)
    return u * hp, hp + (0.5 * RC) * u * (1.0 - t * t) * (1.0 + (3.0 * CC) * u2)


def phase_qkv(x, a1, wqkv, bqkv, g1, s1, qkv):
    def row(r, _):
        rr = rows_of(r)
        n1, _inv = norm(x[rr, :].astype(F))
        a = (n1 * g1[...] + s1[...]).astype(B)
        a1[rr, :] = a
        for t in range(3):
            v = nn(a, wqkv[:, t * D : (t + 1) * D]) + bqkv[:, t * D : (t + 1) * D]
            if t == 0:
                v = v * 0.125
            qkv[rr, t * D : (t + 1) * D] = v.astype(B)
        return 0

    lax.fori_loop(0, T // RT, row, 0)


def pair_attention(hp, n, qkv, o, lse):
    off = pl.multiple_of(hp * 128, 128)
    lane = lax.broadcasted_iota(jnp.int32, (QB, 128), 1)
    for qb in range(T // QB):
        ext = (qb + 1) * QB
        q2 = qkv[pl.ds(qb * QB, QB), pl.ds(off, 128)]
        k2 = qkv[pl.ds(0, ext), pl.ds(D + off, 128)]
        v2 = qkv[pl.ds(0, ext), pl.ds(2 * D + off, 128)]
        key = lax.broadcasted_iota(jnp.int32, (ext, QB), 0)
        qi = lax.broadcasted_iota(jnp.int32, (ext, QB), 1) + qb * QB
        bound = jnp.minimum(qi + 1, n)
        outs = []
        for h in range(2):
            qm = jnp.where((lane // HD) == h, q2, jnp.zeros_like(q2))
            s = jnp.where(key < bound, nt(k2, qm), -1e30)
            m = jnp.max(s, axis=0, keepdims=True)
            e = jnp.exp(s - m)
            l = jnp.sum(e, axis=0, keepdims=True)
            pb = (e * (1.0 / l)).astype(B)
            outs.append(tn(pb, v2))
            lse[pl.ds(hp * 2 + h, 1), pl.ds(qb * QB, QB)] = m + jnp.log(l)
        o[pl.ds(qb * QB, QB), pl.ds(off, 128)] = jnp.where(lane < HD, outs[0], outs[1]).astype(B)


def pair_backward(hp, n, qkv, do, o, lse, dk_s, dv_s, dq_s):
    off = pl.multiple_of(hp * 128, 128)
    lane = lax.broadcasted_iota(jnp.int32, (QB, 128), 1)
    for qb in reversed(range(T // QB)):
        ext = (qb + 1) * QB
        rq = pl.ds(qb * QB, QB)
        q2 = qkv[rq, pl.ds(off, 128)]
        k2 = qkv[pl.ds(0, ext), pl.ds(D + off, 128)]
        v2 = qkv[pl.ds(0, ext), pl.ds(2 * D + off, 128)]
        do2 = do[rq, pl.ds(off, 128)]
        o2 = o[rq, pl.ds(off, 128)]
        prod = (do2.astype(F) * o2.astype(F)).T
        key = lax.broadcasted_iota(jnp.int32, (ext, QB), 0)
        qi = lax.broadcasted_iota(jnp.int32, (ext, QB), 1) + qb * QB
        bound = jnp.minimum(qi + 1, n)
        dqs, dks, dvs = [], [], []
        for h in range(2):
            hm = (lane // HD) == h
            qm = jnp.where(hm, q2, jnp.zeros_like(q2))
            dm = jnp.where(hm, do2, jnp.zeros_like(do2))
            dd = jnp.sum(prod[h * HD : (h + 1) * HD], axis=0, keepdims=True)
            ls = lse[pl.ds(hp * 2 + h, 1), rq]
            p = jnp.where(key < bound, jnp.exp(nt(k2, qm) - ls), 0.0)
            ds = (p * (nt(v2, dm) - dd)).astype(B)
            dqs.append(tn(k2, ds).T)
            dks.append(nn(ds, qm))
            dvs.append(nn(p.astype(B), dm))
        dq_s[rq, :] = (jnp.where(lane < HD, dqs[0], dqs[1]) * 0.125).astype(B)
        dk = dks[0] + dks[1]
        dv = dvs[0] + dvs[1]
        if qb == T // QB - 1:
            dk_s[...] = dk
            dv_s[...] = dv
        else:
            dk_s[pl.ds(0, ext), :] += dk
            dv_s[pl.ds(0, ext), :] += dv
    qkv[:, pl.ds(off, 128)] = dq_s[...]
    qkv[:, pl.ds(D + off, 128)] = dk_s[...].astype(B)
    qkv[:, pl.ds(2 * D + off, 128)] = dv_s[...].astype(B)


def phase_mid(n, x, c, o, wproj, bproj, g2, s2, r1, a2, dm, small):
    def row(r, ob):
        rr = rows_of(r)
        v = x[rr, :].astype(F) + SB * (nn(o[rr, :], wproj[...]) + bproj[...])
        r1[rr, :] = v
        n2, _inv = norm(v)
        a2[rr, :] = (n2 * g2[...] + s2[...]).astype(B)
        ids = lax.broadcasted_iota(jnp.int32, (RT, 1), 0) + r * RT
        cs = SB * (c[rr, :].astype(F) * (ids < n).astype(F))
        dm[rr, :] = cs.astype(B)
        return ob + jnp.sum(cs, axis=0, keepdims=True)

    small[5:6, :] = lax.fori_loop(0, T // RT, row, jnp.zeros((1, D), F))


def mlp_chunk(k, w1, w2, bias, a2, dm, m, da2, hs, dus, gfc, gout, gb):
    tot = jnp.zeros((1, CH), F)
    for r in range(T // RT):
        rr = pl.ds(r * RT, RT)
        u = nn(a2[rr, :], w1[...]) + bias
        h, sl = gelu_pair(u)
        hb = h.astype(B)
        hs[rr, :] = hb
        du = (nt(dm[rr, :], w2[...]) * sl).astype(B)
        dus[rr, :] = du
        m[rr, :] += nn(hb, w2[...])
        da2[rr, :] += nt(du, w1[...])
        tot = tot + jnp.sum(du.astype(F), axis=0, keepdims=True)
    gb[...] = tot
    gout[...] = tn(hs[...], dm[...]).astype(B)
    gfc[...] = tn(a2[...], dus[...]).astype(B)


def phase_back(n, c, r1, m, da2, bout, g2, wproj, dattn, do, out, small):
    def row(r, acc):
        rr = rows_of(r)
        v = r1[rr, :]
        out[rr, :] = (v + SB * (m[rr, :] + bout[...])).astype(B)
        n2, inv = norm(v)
        g = da2[rr, :]
        ids = lax.broadcasted_iota(jnp.int32, (RT, 1), 0) + r * RT
        dr = c[rr, :].astype(F) * (ids < n).astype(F) + norm_back(g * g2[...], n2, inv)
        da2[rr, :] = dr
        sr = SB * dr
        sb = sr.astype(B)
        dattn[rr, :] = sb
        do[rr, :] = nt(sb, wproj[...]).astype(B)
        total = lambda w: jnp.sum(w, axis=0, keepdims=True)
        return acc[0] + total(g * n2), acc[1] + total(g), acc[2] + total(sr)

    z = jnp.zeros((1, D), F)
    a, b, p = lax.fori_loop(0, T // RT, row, (z, z, z))
    small[2:3, :] = p
    small[3:4, :] = a
    small[4:5, :] = b


def phase_end(x, qkv, wqkv, g1, dr1, gin, small):
    def row(r, acc):
        rr = rows_of(r)
        g = nt(qkv[rr, :], wqkv[...])
        n1, inv = norm(x[rr, :].astype(F))
        gin[rr, :] = (dr1[rr, :] + norm_back(g * g1[...], n1, inv)).astype(B)
        total = lambda w: jnp.sum(w, axis=0, keepdims=True)
        return acc[0] + total(g * n1), acc[1] + total(g)

    z = jnp.zeros((1, D), F)
    a, b = lax.fori_loop(0, T // RT, row, (z, z))
    small[0:1, :] = a
    small[1:2, :] = b


def kernel(lens, x, c, g1, s1, wqkv, bqkv, wproj, bproj, g2, s2, wfc, bfc, wout, bout,
           out, gin, gqkv, gproj, gfc, gout, small, gqv, gfcb,
           a1, qkv, o, lse, r1, a2, dm, m, da2, hs, dus, do, dk_s, dv_s, dq_s):
    n = lens[0]
    phase_qkv(x, a1, wqkv, bqkv, g1, s1, qkv)

    def fwd(hp, _):
        pair_attention(hp, n, qkv, o, lse)
        return 0

    lax.fori_loop(0, NP, fwd, 0)
    phase_mid(n, x, c, o, wproj, bproj, g2, s2, r1, a2, dm, small)
    m[...] = jnp.zeros_like(m)
    da2[...] = jnp.zeros_like(da2)

    def chunk(k, _):
        hc = pl.ds(pl.multiple_of(k * CH, CH), CH)
        mlp_chunk(k, wfc.at[k], wout.at[hc], bfc[k], a2, dm, m, da2, hs, dus, gfc.at[k], gout.at[hc], gfcb.at[k])
        return 0

    lax.fori_loop(0, FF // CH, chunk, 0)
    phase_back(n, c, r1, m, da2, bout, g2, wproj, dm, do, out, small)
    gproj[...] = tn(o[...], dm[...]).astype(B)

    def bwd(hp, _):
        pair_backward(hp, n, qkv, do, o, lse, dk_s, dv_s, dq_s)
        off = pl.multiple_of(hp * 128, 128)
        for t in range(3):
            d = qkv[:, pl.ds(t * D + off, 128)]
            gqkv[hp, :, t * 128 : (t + 1) * 128] = tn(a1[...], d).astype(B)
            if t != 1:
                gqv[t // 2 : t // 2 + 1, pl.ds(off, 128)] = jnp.sum(d.astype(F), axis=0, keepdims=True)
        return 0

    lax.fori_loop(0, NP, bwd, 0)
    phase_end(x, qkv, wqkv, g1, da2, gin, small)
    small[6:8, :] = jnp.zeros((2, D), F)


def local_call(*args):
    V = pl.BlockSpec(memory_space=pltpu.VMEM)
    S = pl.BlockSpec(memory_space=pltpu.SMEM)
    sd = jax.ShapeDtypeStruct
    outs = (sd((T, D), B), sd((T, D), B), sd((NP, D, HW), B), sd((D, D), B), sd((FF // CH, D, CH), B),
            sd((FF, D), B), sd((8, D), F), sd((2, D), F), sd((FF // CH, 1, CH), F))
    vm = pltpu.VMEM
    return pl.pallas_call(
        kernel,
        out_shape=outs,
        in_specs=[S] + [V] * 14,
        out_specs=(V, V, V, V, V, V, V, V, V),
        scratch_shapes=[
            vm((T, D), B), vm((T, 3 * D), B), vm((T, D), B), vm((16, T), F), vm((T, D), F), vm((T, D), B),
            vm((T, D), B), vm((T, D), F), vm((T, D), F), vm((T, CH), B), vm((T, CH), B), vm((T, D), B),
            vm((T, 128), F), vm((T, 128), F), vm((T, 128), B),
        ],
        compiler_params=pltpu.CompilerParams(vmem_limit_bytes=62 * 2**20),
    )(*args)


def body(inputs, cotangent, lengths, gain_one, shift_one, qkv_weight, qv_bias, proj_weight, proj_bias, gain_two,
         shift_two, fc_weight, fc_bias, out_weight, out_bias):
    ti = lax.axis_index("tensor")
    swap = lambda v: lax.ppermute(v, "tensor", [(0, 1), (1, 0)])
    pick = lambda v, i: lax.dynamic_index_in_dim(v, i, 0, keepdims=False)

    def whole(v):
        mine = pick(v, ti)[0]
        theirs = swap(pick(v, 1 - ti)[0])
        return jnp.where(ti == 0, jnp.concatenate([mine, theirs]), jnp.concatenate([theirs, mine]))

    x = whole(inputs)
    c = whole(cotangent)
    n = pick(lengths, ti)
    wq = jnp.transpose(qkv_weight, (1, 0, 2))
    wq2 = jnp.stack([wq, swap(wq)], axis=1)
    wqkv = jnp.transpose(wq2, (2, 0, 1, 3)).reshape(D, 3 * D)
    bq = jnp.stack([qv_bias, swap(qv_bias)], axis=1).reshape(2, D)
    bqkv = jnp.concatenate([bq[0], jnp.zeros((D,), F), bq[1]]).reshape(1, 3 * D)
    wproj = jnp.concatenate([proj_weight, swap(proj_weight)])
    chunks = lambda v: jnp.transpose(v.reshape(D, FH // CH, CH), (1, 0, 2))
    wfc = jnp.concatenate([chunks(fc_weight), chunks(swap(fc_weight))])
    bfc = jnp.concatenate([fc_bias, swap(fc_bias)]).reshape(FF // CH, 1, CH)
    wout = jnp.concatenate([out_weight, swap(out_weight)])
    row = lambda v: v.reshape(1, D)
    out, gin, gqkv, gproj, gfc, gout, small, gqv, gfcb = local_call(
        n, x, c, row(gain_one), row(shift_one), wqkv, bqkv, wproj, row(proj_bias), row(gain_two), row(shift_two),
        wfc, bfc, wout, row(out_bias))

    def spread(v):
        half = v.reshape(2, T // 2, D)
        mine = pick(half, ti)
        theirs = swap(pick(half, 1 - ti))
        return jnp.where(ti == 0, jnp.stack([mine, theirs]), jnp.stack([theirs, mine])).astype(F)[:, None]

    def total(v):
        k = v.shape[0] // 2
        return lax.psum(v[:k] + swap(v[k:]), "dp").astype(F)

    gqkv, gproj, gfc, gout = [total(v) for v in (gqkv, gproj, gfc, gout)]
    gqkv = jnp.transpose(gqkv.reshape(3, D, 3, 128), (1, 2, 0, 3)).reshape(D, 3, HW)
    gfc = jnp.transpose(gfc, (1, 0, 2)).reshape(D, FH)
    small = lax.psum(small, ("dp", "tensor"))
    side = jnp.concatenate([gqv.reshape(2, 2, HW), gfcb.reshape(2, 4, HW).transpose(1, 0, 2)])
    side = lax.psum(side[:, 0] + swap(side[:, 1]), "dp")
    return (spread(out), spread(gin), small[0], small[1], gqkv, side[:2], gproj, small[2], small[3], small[4], gfc,
            side[2:].reshape(FH), gout, small[5])


def solution(mesh):
    dp = P(None, "dp", "tensor", None)
    return jax.shard_map(
        body,
        mesh=mesh,
        in_specs=(dp, dp, P(None, "dp"), P(), P(), P(None, None, "tensor"), P(None, "tensor"), P("tensor", None), P(),
                  P(), P(), P(None, "tensor"), P("tensor"), P("tensor", None), P()),
        out_specs=(dp, dp, P(), P(), P(None, None, "tensor"), P(None, "tensor"), P("tensor", None), P(), P(), P(),
                   P(None, "tensor"), P("tensor"), P("tensor", None), P()),
        check_vma=False,
    )
```

```python
import functools

import jax
import jax.numpy as jnp
from jax import lax
from jax.experimental import pallas as pl
from jax.experimental.pallas import tpu as pltpu
from jax.sharding import PartitionSpec as P

F = jnp.float32
B = jnp.bfloat16
T = 1024
D = 768
HD = 64
HW = 384
FF = 3072
FH = 1536
CH = 512
RT = 256
QB = 256
NP = 6
EPS = 1e-05
SB = 48 ** (-0.5)
RC = 0.7978845608028654
CC = 0.044715


def nn(a, b):
    return lax.dot_general(a, b, (((1,), (0,)), ((), ())), preferred_element_type=F)


def nt(a, b):
    return lax.dot_general(a, b, (((1,), (1,)), ((), ())), preferred_element_type=F)


def tn(a, b):
    return lax.dot_general(a, b, (((0,), (0,)), ((), ())), preferred_element_type=F)


def rows_of(r):
    return pl.ds(pl.multiple_of(r * RT, RT), RT)


def norm(v):
    cen = v - jnp.mean(v, axis=-1, keepdims=True)
    inv = lax.rsqrt(jnp.mean(cen * cen, axis=-1, keepdims=True) + EPS)
    return cen * inv, inv


def norm_back(e, n, inv):
    return inv * (e - jnp.mean(e, axis=-1, keepdims=True) - n * jnp.mean(e * n, axis=-1, keepdims=True))


def gelu_pair(u):
    u2 = u * u
    t = jnp.tanh(RC * (u + CC * u2 * u))
    hp = 0.5 * (1.0 + t)
    return u * hp, hp + (0.5 * RC) * u * (1.0 - t * t) * (1.0 + (3.0 * CC) * u2)


def pair_attention(hp, n, qkv, o, lse):
    off = pl.multiple_of(hp * 128, 128)
    lane = lax.broadcasted_iota(jnp.int32, (QB, 128), 1)
    for qb in range(T // QB):
        ext = (qb + 1) * QB
        q2 = qkv[pl.ds(qb * QB, QB), pl.ds(off, 128)]
        k2 = qkv[pl.ds(0, ext), pl.ds(D + off, 128)]
        v2 = qkv[pl.ds(0, ext), pl.ds(2 * D + off, 128)]
        key = lax.broadcasted_iota(jnp.int32, (ext, QB), 0)
        qi = lax.broadcasted_iota(jnp.int32, (ext, QB), 1) + qb * QB
        bound = jnp.minimum(qi + 1, n)
        outs = []
        for h in range(2):
            qm = jnp.where((lane // HD) == h, q2, jnp.zeros_like(q2))
            s = jnp.where(key < bound, nt(k2, qm), -1e30)
            m = jnp.max(s, axis=0, keepdims=True)
            e = jnp.exp(s - m)
            l = jnp.sum(e, axis=0, keepdims=True)
            pb = (e * (1.0 / l)).astype(B)
            outs.append(tn(pb, v2))
            lse[pl.ds(hp * 2 + h, 1), pl.ds(qb * QB, QB)] = m + jnp.log(l)
        o[pl.ds(qb * QB, QB), pl.ds(off, 128)] = jnp.where(lane < HD, outs[0], outs[1]).astype(B)


def pair_backward(hp, n, qkv, do, o, lse, acc):
    off = pl.multiple_of(hp * 128, 128)
    lane = lax.broadcasted_iota(jnp.int32, (QB, 128), 1)
    for qb in reversed(range(T // QB)):
        ext = (qb + 1) * QB
        rq = pl.ds(qb * QB, QB)
        q2 = qkv[rq, pl.ds(off, 128)]
        k2 = qkv[pl.ds(0, ext), pl.ds(D + off, 128)]
        v2 = qkv[pl.ds(0, ext), pl.ds(2 * D + off, 128)]
        do2 = do[rq, pl.ds(off, 128)]
        o2 = o[rq, pl.ds(off, 128)]
        prod = (do2.astype(F) * o2.astype(F)).T
        key = lax.broadcasted_iota(jnp.int32, (ext, QB), 0)
        qi = lax.broadcasted_iota(jnp.int32, (ext, QB), 1) + qb * QB
        bound = jnp.minimum(qi + 1, n)
        dqs, dks, dvs = [], [], []
        for h in range(2):
            hm = (lane // HD) == h
            qm = jnp.where(hm, q2, jnp.zeros_like(q2))
            dm = jnp.where(hm, do2, jnp.zeros_like(do2))
            dd = jnp.sum(prod[h * HD : (h + 1) * HD], axis=0, keepdims=True)
            ls = lse[pl.ds(hp * 2 + h, 1), rq]
            p = jnp.where(key < bound, jnp.exp(nt(k2, qm) - ls), 0.0)
            ds = (p * (nt(v2, dm) - dd)).astype(B)
            dqs.append(tn(k2, ds).T)
            dks.append(nn(ds, qm))
            dvs.append(nn(p.astype(B), dm))
        qkv[rq, pl.ds(off, 128)] = (jnp.where(lane < HD, dqs[0], dqs[1]) * 0.125).astype(B)
        dk = dks[0] + dks[1]
        dv = dvs[0] + dvs[1]
        if qb == T // QB - 1:
            acc[:, 0:128] = dk
            acc[:, 128:256] = dv
        else:
            acc[pl.ds(0, ext), 0:128] += dk
            acc[pl.ds(0, ext), 128:256] += dv
    qkv[:, pl.ds(D + off, 128)] = acc[:, 0:128].astype(B)
    qkv[:, pl.ds(2 * D + off, 128)] = acc[:, 128:256].astype(B)


def phase_mid(n, x, c, o, wproj, bproj, g2, s2, r1, a2, dm, put):
    def row(r, ob):
        rr = rows_of(r)
        v = x[rr, :].astype(F) + SB * (nn(o[rr, :], wproj[...]) + bproj[...])
        r1[rr, :] = v
        n2, _inv = norm(v)
        a2[rr, :] = (n2 * g2[...] + s2[...]).astype(B)
        ids = lax.broadcasted_iota(jnp.int32, (RT, 1), 0) + r * RT
        cs = SB * (c[rr, :].astype(F) * (ids < n).astype(F))
        dm[rr, :] = cs.astype(B)
        return ob + jnp.sum(cs, axis=0, keepdims=True)

    put(5, lax.fori_loop(0, T // RT, row, jnp.zeros((1, D), F)))


def phase_back(n, c, r1, m, da2, bout, g2, wproj, dattn, do, out, put):
    def row(r, acc):
        rr = rows_of(r)
        v = r1[rr, :]
        out[rr, :] = (v + SB * (m[rr, :] + bout[...])).astype(B)
        n2, inv = norm(v)
        g = da2[rr, :]
        ids = lax.broadcasted_iota(jnp.int32, (RT, 1), 0) + r * RT
        dr = c[rr, :].astype(F) * (ids < n).astype(F) + norm_back(g * g2[...], n2, inv)
        da2[rr, :] = dr
        sr = SB * dr
        sb = sr.astype(B)
        dattn[rr, :] = sb
        do[rr, 0:D] = nt(sb, wproj[...]).astype(B)
        total = lambda w: jnp.sum(w, axis=0, keepdims=True)
        return acc[0] + total(g * n2), acc[1] + total(g), acc[2] + total(sr)

    z = jnp.zeros((1, D), F)
    a, b, p = lax.fori_loop(0, T // RT, row, (z, z, z))
    put(2, p)
    put(3, a)
    put(4, b)


def phase_end(x, qkv, wqkv, g1, dr1, gin, put):
    def row(r, acc):
        rr = rows_of(r)
        g = nt(qkv[rr, :], wqkv[...])
        n1, inv = norm(x[rr, :].astype(F))
        gin[rr, :] = (dr1[rr, :] + norm_back(g * g1[...], n1, inv)).astype(B)
        total = lambda w: jnp.sum(w, axis=0, keepdims=True)
        return acc[0] + total(g * n1), acc[1] + total(g)

    z = jnp.zeros((1, D), F)
    a, b = lax.fori_loop(0, T // RT, row, (z, z))
    put(0, a)
    put(1, b)


MESH = pl.DeviceIdType.MESH
NJ = 3
WA = 256
WB = 128
MLP0 = 0
BACK = 6
BWD0 = 7
END = 13


def each(n, fn):
    if n <= 3:
        for d in range(1, n + 1):
            fn(d)
    else:
        lax.fori_loop(1, n + 1, lambda d, _: (fn(d), 0)[1], 0)


def add_rows(rows, dst, srcs):
    step = next(s for s in (192, 128, 64, 32, 16) if rows % s == 0)

    def tile(i, _):
        rr = pl.ds(pl.multiple_of(i * step, step), step)
        v = dst[rr, :].astype(F)
        for s in srcs:
            v = v + s[rr, :].astype(F)
        dst[rr, :] = v.astype(dst.dtype)
        return 0

    lax.fori_loop(0, rows // step, tile, 0)


def depth(dp):
    return (dp // 16 - 1).bit_length()


def mlp_chunk(w1, w2, bias, a2, dm, m, da2, hd, piece):
    tot = jnp.zeros((1, CH), F)
    for r in range(T // RT):
        rr = pl.ds(r * RT, RT)
        u = nn(a2[rr, :], w1[...]) + bias
        h, sl = gelu_pair(u)
        hb = h.astype(B)
        hd[rr, 0:CH] = hb
        du = (nt(dm[rr, :], w2[...]) * sl).astype(B)
        hd[rr, CH : 2 * CH] = du
        m[rr, :] += nn(hb, w2[...])
        da2[rr, :] += nt(du, w1[...])
        tot = tot + jnp.sum(du.astype(F), axis=0, keepdims=True)
    for k in range(D // 256):
        g = tn(a2[:, k * 256 : (k + 1) * 256], hd[:, CH : 2 * CH]).astype(B)
        for b in range(CH // WA):
            piece[b * D + k * 256 : b * D + (k + 1) * 256, :] = g[:, b * WA : (b + 1) * WA]
    base = CH // WA * D
    for k in range(CH // 256):
        g = tn(hd[:, k * 256 : (k + 1) * 256], dm[...]).astype(B)
        for b in range(D // WA):
            piece[base + b * CH + k * 256 : base + b * CH + (k + 1) * 256, :] = g[:, b * WA : (b + 1) * WA]
    return tot


def kernel(dp, lens, inp, cot, g1, s1, wq, bq, wp, bproj, g2, s2, wf, bf, wo, bout,
           out, gin, gq, gp, gf, go, sm, lf, lo,
           xf, cf, a1t, wqkv, wproj, bqo, bfo, wb1, wb2, qkv, o, lse, r1, a2, dm, m, da2, hd,
           pa, ca, xa, ya, za, ga, pb, xb, yb, zb, ps, cs, xs, ys, zs, gs, ss, rs, ls, ready):
    ti = lax.axis_index("tensor")
    me = lax.axis_index("dp")
    nz = 4
    cc = lax.rem(me, 2)
    yy = lax.rem(me // 2, 2)
    zi = lax.rem(me // 4, nz)
    beyond = [{"dp": me + (1 - 2 * lax.rem(me // (16 << b), 2)) * (16 << b)} for b in range(depth(dp))]
    z1 = lax.rem(zi, 2)
    X = {"tensor": 1 - ti}
    C = {"dp": me + 1 - 2 * cc}
    Y = {"dp": me + 2 - 4 * yy}
    Z1 = {"dp": me + 4 - 8 * z1}
    zp = lambda k: {"dp": me + (k - zi) * 4}
    al = pl.multiple_of
    count = [0]
    flags = [0]

    def new(k=1):
        count[0] += k
        return count[0] - k

    def rc(src, dst, i, dev, j=None):
        return pltpu.make_async_remote_copy(src_ref=src, dst_ref=dst, send_sem=ss.at[i], recv_sem=rs.at[i if j is None else j],
                                            device_id=dev, device_id_type=MESH)

    bar = pltpu.get_barrier_semaphore()
    for dev in (X, C, Y):
        pl.semaphore_signal(bar, inc=1, device_id=dev, device_id_type=MESH)
    each(nz - 1, lambda d: pl.semaphore_signal(bar, inc=1, device_id=zp(lax.rem(zi + d, nz)), device_id_type=MESH))
    for dev in beyond:
        pl.semaphore_signal(bar, inc=1, device_id=dev, device_id_type=MESH)
    pl.semaphore_wait(bar, 3 + nz - 1 + len(beyond))

    def units(group):
        if group == 0:
            return [(wq.at[t], lambda r, t=t: wqkv.at[r, t * D + HW : (t + 1) * D], D) for t in range(3)]
        j = group - 1
        cols = slice(j * CH, (j + 1) * CH)
        res = [(wf.at[:, cols], lambda r: lf.at[r, cols], D),
               (wo.at[cols, :], lambda r: lo.at[pl.ds(al(j * CH + r.start, 16), r.size), :], CH)]
        if group == 1:
            res.append((wp, lambda r: wproj.at[pl.ds(al(HW + r.start, 16), r.size), :], HW))
        return res

    wsem = [new(4 * len(units(g))) for g in range(4)]

    def wcopies(group, stage):
        res = []
        for i, (own, land, n) in enumerate(units(group)):
            e = n // 8
            if stage < 2:
                r = pl.ds(al((cc * 4 + yy * 2 + z1) * e, 16), e)
            elif stage == 2:
                r = pl.ds(al((cc * 2 + yy) * 2 * e, 16), 2 * e)
            else:
                r = pl.ds(al(cc * 4 * e, 16), 4 * e)
            src = own.at[r, :] if stage == 0 else land(r)
            res.append(rc(src, land(r), wsem[group] + stage * len(units(group)) + i, (X, Z1, Y, C)[stage]))
        return res

    def wsend(group, stage):
        for c in wcopies(group, stage):
            c.start()

    def wstep(group, stage):
        for c in wcopies(group, stage):
            c.wait()
        if stage < 3:
            wsend(group, stage + 1)

    half = lambda i: pl.ds(al(i * (T // 2), T // 2), T // 2)
    si = new(8)
    x_copy = rc(inp.at[1 - ti], xf.at[half(ti)], si, X)
    c_copy = rc(cot.at[1 - ti], cf.at[half(ti)], si + 1, X)
    bq_copy = rc(bq, bqo, si + 2, X)
    bf_copy = rc(bf, bfo, si + 3, X)
    out_copy = rc(a2.at[half(1 - ti)], out.at[ti], si + 4, X)
    gin_copy = rc(dm.at[half(1 - ti)], gin.at[ti], si + 5, X)
    local = [pltpu.make_async_copy(inp.at[ti], xf.at[half(ti)], ls.at[0]),
             pltpu.make_async_copy(cot.at[ti], cf.at[half(ti)], ls.at[1]),
             pltpu.make_async_copy(wp, wproj.at[0:HW], ls.at[2])]
    local += [pltpu.make_async_copy(wq.at[t], wqkv.at[:, t * D : t * D + HW], ls.at[3 + t]) for t in range(3)]
    wsend(0, 0)
    bq_copy.start()
    x_copy.start()
    for c in local:
        c.start()
    bf_copy.start()
    wsend(1, 0)
    wsend(2, 0)
    c_copy.start()
    wsend(3, 0)

    n = lens[ti, 0]

    def make_set(k_pieces, rows, buf, co, xr, yr, zr, gr, x_first):
        h, q = rows // 2, rows // 4
        s = q // nz
        base = [new(9 + 4 * nz + len(beyond)) for _ in range(k_pieces)]
        flag = flags[0]
        flags[0] += 3 * k_pieces
        mine = al(cc * h, 16)
        keep = al(cc * h + yy * q, 16)
        give = al(cc * h + (1 - yy) * q, 16)
        shard = lambda k: pl.ds(al(keep + k * s, 8), s)

        def swap_c(j):
            r = pl.ds(al((1 - cc) * h, 16), h)
            return [rc(buf(w, j, r), co(j, w), base[j] + w, C) for w in (0, 1)]

        def swap_x(j):
            src = buf(1, j, pl.ds(mine, h)) if x_first else buf(1, j, pl.ds(keep, q))
            return [rc(src, xr.at[j], base[j] + 2, X)]

        def swap_y(j):
            return [rc(buf(w, j, pl.ds(give, q)), yr.at[j, w], base[j] + 3 + w, Y) for w in range(yr.shape[1])]

        def z_out(j):
            each(nz - 1, lambda d: z_one(j, d).start())

        def z_one(j, d):
            k = lax.rem(zi + d, nz)
            return rc(buf(0, j, shard(k)), zr.at[j, zi], base[j] + 9 + k, zp(k), base[j] + 9 + nz + zi)

        def z_in(j):
            def one(d):
                z_one(j, d).wait_send()
                k = lax.rem(zi + d, nz)
                rc(zr.at[j, k], zr.at[j, k], base[j] + 9 + k, zp(k), base[j] + 9 + nz + k).wait_recv()

            each(nz - 1, one)

        def za_one(j, d):
            k = lax.rem(zi + d, nz)
            return rc(buf(0, j, shard(zi)), buf(0, j, shard(zi)), base[j] + 9 + 2 * nz + k, zp(k), base[j] + 9 + 3 * nz + zi)

        def za_in(j):
            def one(d):
                za_one(j, d).wait_send()
                k = lax.rem(zi + d, nz)
                rc(buf(0, j, shard(k)), buf(0, j, shard(k)), base[j] + 9 + 2 * nz + k, zp(k), base[j] + 9 + 3 * nz + k).wait_recv()

            each(nz - 1, one)

        def all_y(j):
            r = pl.ds(keep, q)
            return rc(buf(0, j, r), buf(0, j, r), base[j] + 5, Y)

        def all_c(j):
            r = pl.ds(mine, h)
            return rc(buf(0, j, r), buf(0, j, r), base[j] + 6, C)

        def start(cs):
            for c in cs:
                c.start()

        def wait(cs):
            for c in cs:
                c.wait()

        def free(j, i, dev):
            pl.semaphore_signal(ready.at[flag + 3 * j + i], inc=1, device_id=dev, device_id_type=MESH)

        def freed(j, i, k):
            pl.semaphore_wait(ready.at[flag + 3 * j + i], k)

        def s0(j):
            start(swap_c(j))

        def s1_(j):
            wait(swap_c(j))
            free(j, 0, C)
            for w in (1, 0):
                add_rows(h, buf(w, j, pl.ds(mine, h)), [co(j, w)])
                if w == 1 and x_first:
                    start(swap_x(j))
            if not x_first:
                start(swap_y(j))

        def s2_(j):
            if x_first:
                wait(swap_x(j))
                add_rows(h, buf(0, j, pl.ds(mine, h)), [xr.at[j]])
                start(swap_y(j))
            else:
                wait(swap_y(j))
                free(j, 1, Y)
                for w in (1, 0):
                    add_rows(q, buf(w, j, pl.ds(keep, q)), [yr.at[j, w]])
                    if w == 1:
                        start(swap_x(j))

        def s3_(j):
            if x_first:
                wait(swap_y(j))
                free(j, 1, Y)
                add_rows(q, buf(0, j, pl.ds(keep, q)), [yr.at[j, 0]])
            else:
                wait(swap_x(j))
                add_rows(q, buf(0, j, pl.ds(keep, q)), [xr.at[j]])
            z_out(j)

        def s4_(j):
            z_in(j)
            each(nz - 1, lambda d: free(j, 2, zp(lax.rem(zi + d, nz))))
            add_rows(s, buf(0, j, shard(zi)), [zr.at[j, lax.rem(zi + d, nz)] for d in range(1, nz)])
            for b, dev in enumerate(beyond):
                copy = rc(buf(0, j, shard(zi)), gr(j, b), base[j] + 9 + 4 * nz + b, dev)
                copy.start()
                copy.wait()
                add_rows(s, buf(0, j, shard(zi)), [gr(j, b)])
            freed(j, 2, nz - 1)
            each(nz - 1, lambda d: za_one(j, d).start())

        def s5_(j):
            za_in(j)
            freed(j, 1, 1)
            all_y(j).start()

        def s6_(j):
            all_y(j).wait()
            freed(j, 0, 1)
            all_c(j).start()

        def s7_(j):
            all_c(j).wait()

        return [s0, s1_, s2_, s3_, s4_, s5_, s6_, s7_]

    ra = pa.shape[2]
    lanes = slice(0, WB)
    set_a = make_set(NJ, ra, lambda w, j, r: pa.at[w, j, r], lambda j, w: ca.at[j, w], xa, ya, za, lambda j, b: ga.at[j % 2, b], True)
    buf_b = lambda w, j, r: pa.at[1, j, r, lanes] if w else pb.at[j, r]
    set_b = make_set(NJ, ra, buf_b, lambda j, w: ca.at[j, w, :, lanes], xb, yb, zb, lambda j, b: ga.at[(j + 1) % 2, b, :, lanes], False)
    set_s = make_set(1, ps.shape[2], lambda w, j, r: ps.at[w, j, r], lambda j, w: cs.at[j, w], xs, ys, zs, lambda j, b: gs.at[0, b], False)

    def out_a(j):
        own = pa.at[0, j]
        res = [(own.at[b * D : (b + 1) * D], gf.at[:, j * CH + b * WA : j * CH + (b + 1) * WA]) for b in range(CH // WA)]
        base = CH // WA * D
        res += [(own.at[base + b * CH : base + (b + 1) * CH], go.at[j * CH : (j + 1) * CH, b * WA : (b + 1) * WA])
                for b in range(D // WA)]
        return [pltpu.make_async_copy(u, v, ls.at[8 + j * 5 + i]) for i, (u, v) in enumerate(res)]

    def out_b(j):
        own = pb.at[j]
        res = [(own.at[t * D : (t + 1) * D], gq.at[t, :, j * WB : (j + 1) * WB]) for t in range(3)]
        res += [(own.at[3 * D + b * WB : 3 * D + (b + 1) * WB], gp.at[j * WB : (j + 1) * WB, b * WB : (b + 1) * WB])
                for b in range(D // WB)]
        return [pltpu.make_async_copy(u, v, ls.at[23 + j * 9 + i]) for i, (u, v) in enumerate(res)]

    def a_step(j, s):
        def run():
            set_a[s](j)
            if s == 7:
                for c in out_a(j):
                    c.start()
        return run

    def b_step(j, s):
        def run():
            set_b[s](j)
            if s == 7:
                for c in out_b(j):
                    c.start()
        return run

    events = {}

    def at(tick, fn):
        events.setdefault(tick, []).append(fn)

    a_ticks = [[1, 2, 6, 8, 10, 12], [3, 4, 8, 10, 12, 13], [5, 6, 11, 13]]
    b_ticks = [[8, 9, 11, 13], [10, 11, 13], [12, 13]]
    pos_a, pos_b = [], []
    for j in range(NJ):
        for s, tick in enumerate(a_ticks[j]):
            at(tick, a_step(j, s))
        for s, tick in enumerate(b_ticks[j]):
            at(tick, b_step(j, s))
        pos_a.append(len(a_ticks[j]))
        pos_b.append(len(b_ticks[j]))

    def ticks(first, last, t):
        for g in range(first, last):
            if g in events:
                @pl.when(t + first == g)
                def _(g=g):
                    for fn in events[g]:
                        fn()

    def put(i, v):
        for w in (0, 1):
            for b in range(D // 128):
                ps[w, 0, i * 8 + b : i * 8 + b + 1, :] = v[:, b * 128 : (b + 1) * 128]

    ps[...] = jnp.zeros_like(ps)

    wstep(0, 0)
    wstep(0, 1)
    local[0].wait()
    x_copy.wait()

    def ln_row(r, _):
        rr = rows_of(r)
        n1, _inv = norm(xf[rr, :].astype(F))
        a = (n1 * g1[...] + s1[...]).astype(B)
        a2[rr, :] = a
        a1t[:, rr] = a.T
        return 0

    lax.fori_loop(0, T // RT, ln_row, 0)
    wstep(0, 2)
    bq_copy.wait()
    for c in local[3:]:
        c.wait()
    wstep(0, 3)
    wstep(1, 0)

    def qkv_row(r, _):
        rr = rows_of(r)
        a = a2[rr, :]
        for t in range(3):
            v = nn(a, wqkv[:, t * D : (t + 1) * D])
            for k, b in enumerate((bq, bqo)):
                u = v[:, k * HW : (k + 1) * HW]
                if t != 1:
                    u = u + b[t // 2 : t // 2 + 1, :]
                if t == 0:
                    u = u * 0.125
                qkv[rr, t * D + k * HW : t * D + (k + 1) * HW] = u.astype(B)
        return 0

    lax.fori_loop(0, T // RT, qkv_row, 0)

    def fwd(hp, _):
        pair_attention(hp, n, qkv, o, lse)
        for t, fns in ((1, [(1, 1), (2, 0)]), (3, [(2, 1)]), (4, [(1, 2)])):
            @pl.when(hp == t)
            def _(fns=fns):
                for f in fns:
                    wstep(*f)
        return 0

    lax.fori_loop(0, NP, fwd, 0)
    local[1].wait()
    local[2].wait()
    wstep(1, 3)
    c_copy.wait()
    bf_copy.wait()

    def fetch(which, j):
        cols = pl.ds(al(j * CH, CH), CH)
        s1 = (wf if which == 0 else lf).at[:, cols]
        s2 = (wo if which == 0 else lo).at[cols, :]
        return [pltpu.make_async_copy(s1, wb1.at[which], ls.at[50 + which]),
                pltpu.make_async_copy(s2, wb2.at[which], ls.at[52 + which])]

    for c in fetch(0, 0):
        c.start()
    phase_mid(n, xf, cf, o, wproj, bproj, g2, s2, r1, a2, dm, put)
    m[...] = jnp.zeros_like(m)
    da2[...] = jnp.zeros_like(da2)

    def chunk(t, _):
        which = lax.rem(t, 2)
        j = t // 2
        for g, fns in ((0, [(2, 2), (3, 0)]), (1, [(2, 3), (3, 1)]), (3, [(3, 2)]), (4, [(3, 3)])):
            @pl.when(t == g)
            def _(fns=fns):
                for f in fns:
                    wstep(*f)
        for w in (0, 1):
            @pl.when(which == w)
            def _(w=w):
                for c in fetch(w, j):
                    c.wait()

            @pl.when((which == 1 - w) & (t < 5))
            def _(w=w):
                for c in fetch(w, (t + 1) // 2):
                    c.start()
        bias = jnp.where(which == 0, bf[j], bfo[j])
        tot = mlp_chunk(wb1.at[which], wb2.at[which], bias, a2, dm, m, da2, hd, pa.at[which, j])
        for b in range(CH // 128):
            ps[which, 0, pl.ds(64 + j * 4 + b, 1), :] = tot[:, b * 128 : (b + 1) * 128]
        ticks(0, 6, t)
        return 0

    lax.fori_loop(0, 6, chunk, 0)

    phase_back(n, cf, r1, m, da2, bout, g2, wproj, dm, hd, a2, put)
    for fn in events[6]:
        fn()
    out_copy.start()
    out_own = pltpu.make_async_copy(a2.at[half(ti)], out.at[ti], ls.at[6])
    gin_own = pltpu.make_async_copy(dm.at[half(ti)], gin.at[ti], ls.at[7])
    out_own.start()

    def bwd(t, _):
        which = lax.rem(t, 2)
        j = t // 2
        hp = which * NJ + j
        pair_backward(hp, n, qkv, hd, o, lse, m)
        off = al(hp * 128, 128)
        d = jnp.concatenate([qkv[:, pl.ds(k * D + off, 128)] for k in range(3)], axis=1)
        g = nn(a1t[...], d).astype(B)
        e = tn(o[:, pl.ds(off, 128)], dm[...]).astype(B)

        def store(piece):
            for k in range(3):
                piece[k * D : (k + 1) * D, :] = g[:, k * 128 : (k + 1) * 128]
            for b in range(D // WB):
                piece[3 * D + b * WB : 3 * D + (b + 1) * WB, :] = e[:, b * WB : (b + 1) * WB]

        @pl.when(which == 0)
        def _():
            store(pb.at[j])

        @pl.when(which == 1)
        def _():
            store(pa.at[1, j, :, lanes])

        for k, base in ((0, 48), (2, 56)):
            v = jnp.sum(qkv[:, pl.ds(k * D + off, 128)].astype(F), axis=0, keepdims=True)
            ps[which, 0, pl.ds(base + j, 1), :] = v
        ticks(7, 13, t)
        return 0

    lax.fori_loop(0, 6, bwd, 0)
    phase_end(xf, qkv, wqkv, g1, da2, dm, put)
    set_s[0](0)
    gin_copy.start()
    gin_own.start()
    for fn in events[13]:
        fn()
    pos_s = 1
    for rnd in range(8):
        for j in range(NJ):
            if pos_a[j] < 8:
                a_step(j, pos_a[j])()
                pos_a[j] += 1
        for j in range(NJ):
            if pos_b[j] < 8:
                b_step(j, pos_b[j])()
                pos_b[j] += 1
        if pos_s < 8:
            set_s[pos_s](0)
            pos_s += 1
    sm_own = pltpu.make_async_copy(ps.at[0, 0], sm, ls.at[54])
    sm_own.start()
    for j in range(NJ):
        for c in out_a(j) + out_b(j):
            c.wait()
    for c in (sm_own, out_own, gin_own, out_copy, gin_copy):
        c.wait()
    assert count[0] <= SEMS(dp)


def SEMS(dp):
    return 48 + 7 * (25 + depth(dp))


def local_call(dp, *args):
    V = pl.BlockSpec(memory_space=pltpu.VMEM)
    S = pl.BlockSpec(memory_space=pltpu.SMEM)
    A = pl.BlockSpec(memory_space=pl.ANY)
    sd = jax.ShapeDtypeStruct
    ra, rsm, nz = 4 * D, 256, 4
    nb = max(depth(dp), 1)
    outs = (sd((2, T // 2, D), B), sd((2, T // 2, D), B), sd((3, D, HW), B), sd((HW, D), B), sd((D, FH), B),
            sd((FH, D), B), sd((rsm, 128), F), sd((D, FH), B), sd((FH, D), B))
    vm = pltpu.VMEM
    sem = pltpu.SemaphoreType.DMA

    def buffers(k, r, w, x_first, dt):
        return [vm((2, k, r, w), dt), vm((k, 2, r // 2, w), dt), vm((k, r // 2 if x_first else r // 4, w), dt),
                vm((k, 1 if x_first else 2, r // 4, w), dt), vm((k, nz, r // 4 // nz, w), dt), vm((min(k, 2), nb, r // 4 // nz, w) if dp > 16 else (1, 1, 16, 128), dt)]

    return pl.pallas_call(
        functools.partial(kernel, dp),
        out_shape=outs,
        in_specs=[S, A, A, V, V, A, V, A, V, V, V, A, V, A, V],
        out_specs=(A,) * 9,
        scratch_shapes=[
            vm((T, D), B), vm((T, D), B), vm((D, T), B), vm((D, 3 * D), B), vm((D, D), B), vm((2, HW), F), vm((3, 1, CH), F),
            vm((2, D, CH), B), vm((2, CH, D), B), vm((T, 3 * D), B), vm((T, D), B), vm((16, T), F), vm((T, D), F),
            vm((T, D), B), vm((T, D), B), vm((T, D), F), vm((T, D), F), vm((T, 2 * CH), B),
        ] + buffers(NJ, ra, WA, True, B) + [vm((NJ, ra, WB), B)] + buffers(NJ, ra, WB, False, B)[2:5] + buffers(1, rsm, 128, False, F)
        + [sem((SEMS(dp),)), sem((SEMS(dp),)), sem((56,)), pltpu.SemaphoreType.REGULAR((21,))],
        compiler_params=pltpu.CompilerParams(vmem_limit_bytes=VLIMIT, collective_id=0, has_side_effects=True),
    )(*args)


VLIMIT = 63 * 2**20 + 2**19


def body(dp, inputs, cotangent, lengths, gain_one, shift_one, qkv_weight, qv_bias, proj_weight, proj_bias, gain_two,
         shift_two, fc_weight, fc_bias, out_weight, out_bias):
    row = lambda v: v.reshape(1, D)
    out, gin, gq, gp, gf, go, sm, _lf, _lo = local_call(
        dp, lengths, inputs.reshape(2, T // 2, D), cotangent.reshape(2, T // 2, D), row(gain_one), row(shift_one),
        jnp.transpose(qkv_weight, (1, 0, 2)), qv_bias, proj_weight, row(proj_bias), row(gain_two), row(shift_two),
        fc_weight, fc_bias.reshape(3, 1, CH), out_weight, row(out_bias))
    vec = lambda i: sm[i * 8 : i * 8 + 6].reshape(D)
    gqv = jnp.stack([sm[48:51].reshape(HW), sm[56:59].reshape(HW)])
    rows = lambda v: v.astype(F)[:, None]
    return (rows(out), rows(gin), vec(0), vec(1), jnp.transpose(gq.astype(F), (1, 0, 2)), gqv, gp.astype(F), vec(2), vec(3),
            vec(4), gf.astype(F), sm[64:76].reshape(FH), go.astype(F), vec(5))


def solution(mesh):
    dp = P(None, "dp", "tensor", None)
    return jax.shard_map(
        functools.partial(body, mesh.shape["dp"]),
        mesh=mesh,
        in_specs=(dp, dp, P(None, "dp"), P(), P(), P(None, None, "tensor"), P(None, "tensor"), P("tensor", None), P(),
                  P(), P(), P(None, "tensor"), P("tensor"), P("tensor", None), P()),
        out_specs=(dp, dp, P(), P(), P(None, None, "tensor"), P(None, "tensor"), P("tensor", None), P(), P(), P(),
                   P(None, "tensor"), P("tensor"), P("tensor", None), P()),
        check_vma=False,
    )
```

```python
import functools

import jax
import jax.numpy as jnp
from jax import lax
from jax.experimental import pallas as pl
from jax.experimental.pallas import tpu as pltpu
from jax.sharding import PartitionSpec as P

F = jnp.float32
B = jnp.bfloat16
T = 1024
D = 768
HD = 64
HW = 384
FF = 3072
FH = 1536
CH = 512
RT = 256
QB = 256
NP = 6
EPS = 1e-05
SB = 48 ** (-0.5)
RC = 0.7978845608028654
CC = 0.044715


def nn(a, b):
    return lax.dot_general(a, b, (((1,), (0,)), ((), ())), preferred_element_type=F)


def nt(a, b):
    return lax.dot_general(a, b, (((1,), (1,)), ((), ())), preferred_element_type=F)


def tn(a, b):
    return lax.dot_general(a, b, (((0,), (0,)), ((), ())), preferred_element_type=F)


def rows_of(r):
    return pl.ds(pl.multiple_of(r * RT, RT), RT)


def norm(v):
    cen = v - jnp.mean(v, axis=-1, keepdims=True)
    inv = lax.rsqrt(jnp.mean(cen * cen, axis=-1, keepdims=True) + EPS)
    return cen * inv, inv


def norm_back(e, n, inv):
    return inv * (e - jnp.mean(e, axis=-1, keepdims=True) - n * jnp.mean(e * n, axis=-1, keepdims=True))


def gelu_pair(u):
    u2 = u * u
    t = jnp.tanh(RC * (u + CC * u2 * u))
    hp = 0.5 * (1.0 + t)
    return u * hp, hp + (0.5 * RC) * u * (1.0 - t * t) * (1.0 + (3.0 * CC) * u2)


def pair_attention(hp, n, qkv, o, lse):
    off = pl.multiple_of(hp * 128, 128)
    lane = lax.broadcasted_iota(jnp.int32, (QB, 128), 1)
    for qb in range(T // QB):
        ext = (qb + 1) * QB
        q2 = qkv[pl.ds(qb * QB, QB), pl.ds(off, 128)]
        k2 = qkv[pl.ds(0, ext), pl.ds(D + off, 128)]
        v2 = qkv[pl.ds(0, ext), pl.ds(2 * D + off, 128)]
        key = lax.broadcasted_iota(jnp.int32, (ext, QB), 0)
        qi = lax.broadcasted_iota(jnp.int32, (ext, QB), 1) + qb * QB
        bound = jnp.minimum(qi + 1, n)
        outs = []
        for h in range(2):
            qm = jnp.where((lane // HD) == h, q2, jnp.zeros_like(q2))
            s = jnp.where(key < bound, nt(k2, qm), -1e30)
            m = jnp.max(s, axis=0, keepdims=True)
            e = jnp.exp(s - m)
            l = jnp.sum(e, axis=0, keepdims=True)
            pb = (e * (1.0 / l)).astype(B)
            outs.append(tn(pb, v2))
            lse[pl.ds(hp * 2 + h, 1), pl.ds(qb * QB, QB)] = m + jnp.log(l)
        o[pl.ds(qb * QB, QB), pl.ds(off, 128)] = jnp.where(lane < HD, outs[0], outs[1]).astype(B)


def pair_backward(hp, n, qkv, do, o, lse, acc):
    off = pl.multiple_of(hp * 128, 128)
    lane = lax.broadcasted_iota(jnp.int32, (QB, 128), 1)
    for qb in reversed(range(T // QB)):
        ext = (qb + 1) * QB
        rq = pl.ds(qb * QB, QB)
        q2 = qkv[rq, pl.ds(off, 128)]
        k2 = qkv[pl.ds(0, ext), pl.ds(D + off, 128)]
        v2 = qkv[pl.ds(0, ext), pl.ds(2 * D + off, 128)]
        do2 = do[rq, pl.ds(off, 128)]
        o2 = o[rq, pl.ds(off, 128)]
        prod = (do2.astype(F) * o2.astype(F)).T
        key = lax.broadcasted_iota(jnp.int32, (ext, QB), 0)
        qi = lax.broadcasted_iota(jnp.int32, (ext, QB), 1) + qb * QB
        bound = jnp.minimum(qi + 1, n)
        dqs, dks, dvs = [], [], []
        for h in range(2):
            hm = (lane // HD) == h
            qm = jnp.where(hm, q2, jnp.zeros_like(q2))
            dm = jnp.where(hm, do2, jnp.zeros_like(do2))
            dd = jnp.sum(prod[h * HD : (h + 1) * HD], axis=0, keepdims=True)
            ls = lse[pl.ds(hp * 2 + h, 1), rq]
            p = jnp.where(key < bound, jnp.exp(nt(k2, qm) - ls), 0.0)
            ds = (p * (nt(v2, dm) - dd)).astype(B)
            dqs.append(tn(k2, ds).T)
            dks.append(nn(ds, qm))
            dvs.append(nn(p.astype(B), dm))
        qkv[rq, pl.ds(off, 128)] = (jnp.where(lane < HD, dqs[0], dqs[1]) * 0.125).astype(B)
        dk = dks[0] + dks[1]
        dv = dvs[0] + dvs[1]
        if qb == T // QB - 1:
            acc[:, 0:128] = dk
            acc[:, 128:256] = dv
        else:
            acc[pl.ds(0, ext), 0:128] += dk
            acc[pl.ds(0, ext), 128:256] += dv
    qkv[:, pl.ds(D + off, 128)] = acc[:, 0:128].astype(B)
    qkv[:, pl.ds(2 * D + off, 128)] = acc[:, 128:256].astype(B)


def phase_mid(n, x, c, o, wproj, bproj, g2, s2, r1, a2, dm, put):
    def row(r, ob):
        rr = rows_of(r)
        v = x[rr, :].astype(F) + SB * (nn(o[rr, :], wproj[...]) + bproj[...])
        r1[rr, :] = v
        n2, _inv = norm(v)
        a2[rr, :] = (n2 * g2[...] + s2[...]).astype(B)
        ids = lax.broadcasted_iota(jnp.int32, (RT, 1), 0) + r * RT
        cs = SB * (c[rr, :].astype(F) * (ids < n).astype(F))
        dm[rr, :] = cs.astype(B)
        return ob + jnp.sum(cs, axis=0, keepdims=True)

    put(5, lax.fori_loop(0, T // RT, row, jnp.zeros((1, D), F)))


def phase_back(n, c, r1, m, da2, bout, g2, wproj, dattn, do, out, put):
    def row(r, acc):
        rr = rows_of(r)
        v = r1[rr, :]
        out[rr, :] = (v + SB * (m[rr, :] + bout[...])).astype(B)
        n2, inv = norm(v)
        g = da2[rr, :]
        ids = lax.broadcasted_iota(jnp.int32, (RT, 1), 0) + r * RT
        dr = c[rr, :].astype(F) * (ids < n).astype(F) + norm_back(g * g2[...], n2, inv)
        da2[rr, :] = dr
        sr = SB * dr
        sb = sr.astype(B)
        dattn[rr, :] = sb
        do[rr, 0:D] = nt(sb, wproj[...]).astype(B)
        total = lambda w: jnp.sum(w, axis=0, keepdims=True)
        return acc[0] + total(g * n2), acc[1] + total(g), acc[2] + total(sr)

    z = jnp.zeros((1, D), F)
    a, b, p = lax.fori_loop(0, T // RT, row, (z, z, z))
    put(2, p)
    put(3, a)
    put(4, b)


def phase_end(x, qkv, wqkv, g1, dr1, gin, first, sums):
    def row(r, acc):
        rr = rows_of(r)
        g = nt(qkv[rr, :], wqkv[...])
        n1, inv = norm(x[rr, :].astype(F))
        gin[rr, :] = (dr1[rr, :] + norm_back(g * g1[...], n1, inv)).astype(B)
        total = lambda w: jnp.sum(w, axis=0, keepdims=True)
        return acc[0] + total(g * n1), acc[1] + total(g)

    z = jnp.zeros((1, D), F)
    return lax.fori_loop(first, first + T // RT // 2, row, (z, z) if sums is None else sums)


EVENTS = {
    "ln": (),
    "q0": ("W4.w0",),
    "q1": (),
    "q2": (),
    "q3": (),
    "f0": ("W1.w0", "W4.w1",),
    "f1": ("W2.w0",),
    "f2": ("W1.w1", "W4.w2",),
    "f3": ("W2.w1", "W4.w3",),
    "f4": (),
    "f5": ("W1.w2",),
    "mid0": (),
    "mid1": ("W3.w0", "W2.w2",),
    "mid2": ("W1.w3",),
    "m0a": (),
    "m0b": ("A0.cs1", "W3.w1", "W2.w3",),
    "m1a": ("A0.cd1",),
    "m1b": ("A0.cs0",),
    "m2a": ("W3.w2", "A0.cd0",),
    "m2b": ("A1.cs1",),
    "m3a": ("W3.w3", "A0.yd1",),
    "m3b": ("A1.cs0", "A1.cd1",),
    "m4a": ("A0.yd0",),
    "m4b": ("A2.cs1", "A1.cd0",),
    "m5a": ("A0.xd",),
    "m5b": ("A2.cs0", "A1.yd1", "A2.cd1",),
    "back": ("A2.cd0",),
    "b0a": ("out0", "A1.yd0", "A1.xd",),
    "b0b": ("B0.cs1", "A0.zd",),
    "b1a": ("out1", "A2.yd1", "B0.cd1",),
    "b1b": ("B0.cs0",),
    "b2a": ("A1.zd",),
    "b2b": ("B1.cs1",),
    "b3a": ("out2", "B0.cd0", "A2.yd0", "B0.yd1", "A0.zad",),
    "b3b": ("B1.cs0", "B1.cd1", "A2.xd",),
    "b4a": ("B1.cd0", "B0.yd0", "A1.zad",),
    "b4b": ("B2.cs1", "B0.xd",),
    "b5a": ("B2.cd1", "A2.zd", "A0.yad",),
    "b5b": ("B2.cs0",),
    "end1": ("B1.xd", "B0.zd",),
    "end1b": (),
    "end2": ("S.cs1", "S.cs0", "S.cd1", "out3", "B2.cd0", "B2.xd", "A2.zad", "S.yd1", "S.cd0", "B1.yd0",
        "A1.yad", "gin0", "A0.cad",),
    "drain": ("B0.zad", "B2.yd0", "A1.cad", "gin1", "B1.zd", "gin2", "B2.zd", "A2.yad", "S.yd0", "gin3", "S.xd",
        "B1.zad", "B0.yad", "A2.cad", "B2.zad", "S.zd", "B0.cad", "B1.yad", "S.zad", "B1.cad", "B2.yad", "S.yad",
        "B2.cad", "S.cad",),
}
WAY = ("yz", "zy", "yz", "yz", "zy")
XA = (False, False, False)
XB = (False, True, True)
FIRST = "oth"
COUNT = 4
ORDER = "mix"
MESH = pl.DeviceIdType.MESH
NJ = 3
WA = 256
WB = 128


def each(n, fn):
    if n <= 3:
        for d in range(1, n + 1):
            fn(d)
    else:
        lax.fori_loop(1, n + 1, lambda d, _: (fn(d), 0)[1], 0)


def add_rows(rows, dst, srcs):
    step = next(s for s in (192, 128, 64, 32, 16) if rows % s == 0)

    def tile(i, _):
        rr = pl.ds(pl.multiple_of(i * step, step), step)
        v = dst[rr, :].astype(F)
        for s in srcs:
            v = v + s[rr, :].astype(F)
        dst[rr, :] = v.astype(dst.dtype)
        return 0

    lax.fori_loop(0, rows // step, tile, 0)


def depth(dp):
    return (dp // 16 - 1).bit_length()


def mlp_rows(w1, w2, bias, a2, dm, m, da2, hd):
    tot = jnp.zeros((1, CH), F)
    for r in range(T // RT):
        rr = pl.ds(r * RT, RT)
        u = nn(a2[rr, :], w1[...]) + bias
        h, sl = gelu_pair(u)
        hb = h.astype(B)
        hd[rr, 0:CH] = hb
        du = (nt(dm[rr, :], w2[...]) * sl).astype(B)
        hd[rr, CH : 2 * CH] = du
        m[rr, :] += nn(hb, w2[...])
        da2[rr, :] += nt(du, w1[...])
        tot = tot + jnp.sum(du.astype(F), axis=0, keepdims=True)
    return tot


def mlp_grads(a2, dm, hd, piece):
    for k in range(D // 256):
        g = tn(a2[:, k * 256 : (k + 1) * 256], hd[:, CH : 2 * CH]).astype(B)
        for b in range(CH // WA):
            piece[b * D + k * 256 : b * D + (k + 1) * 256, :] = g[:, b * WA : (b + 1) * WA]
    base = CH // WA * D
    for k in range(CH // 256):
        g = tn(hd[:, k * 256 : (k + 1) * 256], dm[...]).astype(B)
        for b in range(D // WA):
            piece[base + b * CH + k * 256 : base + b * CH + (k + 1) * 256, :] = g[:, b * WA : (b + 1) * WA]


class Row:
    def __init__(self, ref):
        self.ref = ref

    def __getitem__(self, _):
        return self.ref[...].reshape(1, -1)


def kernel(dp, lens, inp, cot, wq, bq, wp, wf, wo, g1, s1, bproj, g2, s2, bout, fcb,
           out, gin, gq, gp, gf, go, sm, lf, lo,
           xf, cf, a1t, wqkv, wproj, bqo, bfm, bfo, wb1, wb2, qkv, o, lse, r1, a2, dm, m, da2, hd,
           pa, ca, xa, ya, za, ga, pb, xb, yb, zb, ps, cs, xs, ys, zs, gs, ss, rs, ls, ready):
    g1, s1, bproj, g2, s2, bout = (Row(v) for v in (g1, s1, bproj, g2, s2, bout))
    ti = lax.axis_index("tensor")
    me = lax.axis_index("dp")
    nz = 4
    cc = lax.rem(me, 2)
    yy = lax.rem(me // 2, 2)
    zi = lax.rem(me // 4, nz)
    beyond = [{"dp": me + (1 - 2 * lax.rem(me // (16 << b), 2)) * (16 << b)} for b in range(depth(dp))]
    z1 = lax.rem(zi, 2)
    X = {"tensor": 1 - ti}
    C = {"dp": me + 1 - 2 * cc}
    Y = {"dp": me + 2 - 4 * yy}
    Z1 = {"dp": me + 4 - 8 * z1}
    zp = lambda k: {"dp": me + (k - zi) * 4}
    al = pl.multiple_of
    count = [0]
    flags = [0]

    def new(k=1):
        count[0] += k
        return count[0] - k

    def rc(src, dst, i, dev, j=None):
        return pltpu.make_async_remote_copy(src_ref=src, dst_ref=dst, send_sem=ss.at[i], recv_sem=rs.at[i if j is None else j],
                                            device_id=dev, device_id_type=MESH)

    bar = pltpu.get_barrier_semaphore()
    for dev in (X, C, Y):
        pl.semaphore_signal(bar, inc=1, device_id=dev, device_id_type=MESH)
    each(nz - 1, lambda d: pl.semaphore_signal(bar, inc=1, device_id=zp(lax.rem(zi + d, nz)), device_id_type=MESH))
    for dev in beyond:
        pl.semaphore_signal(bar, inc=1, device_id=dev, device_id_type=MESH)
    pl.semaphore_wait(bar, 3 + nz - 1 + len(beyond))

    def units(group):
        if group == 0:
            return [(wq.at[t], lambda r, t=t: wqkv.at[r, t * D + HW : (t + 1) * D], D) for t in range(3)]
        if group == 4:
            return [(wp, lambda r: wproj.at[pl.ds(al(HW + r.start, 16), r.size), :], HW)]
        j = group - 1
        cols = slice(j * CH, (j + 1) * CH)
        return [(wf.at[:, cols], lambda r: lf.at[r, cols], D),
                (wo.at[cols, :], lambda r: lo.at[pl.ds(al(j * CH + r.start, 16), r.size), :], CH)]

    wsem = [new(4 * len(units(g))) for g in range(5)]

    def wcopies(group, stage):
        res = []
        first, second = ((z1, Z1), (yy, Y))[:: 1 if WAY[group] == "zy" else -1]
        for i, (own, land, n) in enumerate(units(group)):
            e = n // 8
            if stage < 2:
                r = pl.ds(al((cc * 4 + second[0] * 2 + first[0]) * e, 16), e)
            elif stage == 2:
                r = pl.ds(al((cc * 2 + second[0]) * 2 * e, 16), 2 * e)
            else:
                r = pl.ds(al(cc * 4 * e, 16), 4 * e)
            src = own.at[r, :] if stage == 0 else land(r)
            dev = (X, first[1], second[1], C)[stage]
            res.append(rc(src, land(r), wsem[group] + stage * len(units(group)) + i, dev))
        return res

    def wsend(group, stage):
        for c in wcopies(group, stage):
            c.start()

    def wstep(group, stage):
        nexts = wcopies(group, stage + 1) if stage < 3 else [None] * len(units(group))
        for c, d in zip(wcopies(group, stage), nexts):
            c.wait()
            if d is not None:
                d.start()

    half = lambda i: pl.ds(al(i * (T // 2), T // 2), T // 2)
    si = new(12)
    x_copy = rc(inp.at[1 - ti], xf.at[half(ti)], si, X)
    c_copy = rc(cot.at[1 - ti], cf.at[half(ti)], si + 1, X)
    bq_copy = rc(bq, bqo, si + 2, X)
    bf_copy = rc(bfm, bfo, si + 3, X)
    def rows_back(v, res, i):
        q = T // 2 // COUNT
        there = lambda b, k: pl.ds(al(b * (T // 2) + k * q, 16), q)
        return [rc(v.at[there(1 - ti, k)], res.at[ti, k * q : (k + 1) * q], si + i + k, X) for k in range(COUNT)]

    out_copy = rows_back(a2, out, 4)
    gin_copy = rows_back(dm, gin, 8)
    local = [pltpu.make_async_copy(inp.at[ti], xf.at[half(ti)], ls.at[0]),
             pltpu.make_async_copy(cot.at[ti], cf.at[half(ti)], ls.at[1]),
             pltpu.make_async_copy(wp, wproj.at[0:HW], ls.at[2])]
    local += [pltpu.make_async_copy(wq.at[t], wqkv.at[:, t * D : t * D + HW], ls.at[3 + t]) for t in range(3)]
    wsend(0, 0)
    bq_copy.start()
    x_copy.start()
    for c in local:
        c.start()

    n = lens[0, ti]
    for j in range(NJ):
        bfm[j : j + 1, :] = fcb[j * CH : (j + 1) * CH].reshape(1, CH)
    bfm[NJ:, :] = jnp.zeros((8 - NJ, CH), F)

    def make_set(k_pieces, rows, buf, co, xr, yr, zr, gr, xs_first):
        h, q = rows // 2, rows // 4
        s = q // nz
        base = [new(9 + 4 * nz + len(beyond)) for _ in range(k_pieces)]
        flag = flags[0]
        flags[0] += 3 * k_pieces
        mine = al(cc * h, 16)
        keep = al(cc * h + yy * q, 16)
        give = al(cc * h + (1 - yy) * q, 16)
        shard = lambda k: pl.ds(al(keep + k * s, 8), s)

        def swap_c(j, w):
            return rc(buf(w, j, pl.ds(al((1 - cc) * h, 16), h)), co(j, w), base[j] + w, C)

        def swap_x(j):
            src = buf(1, j, pl.ds(mine, h)) if xs_first[j] else buf(1, j, pl.ds(keep, q))
            return rc(src, xr(j), base[j] + 2, X)

        def swap_y(j, w):
            return rc(buf(w, j, pl.ds(give, q)), yr(j, w), base[j] + 3 + w, Y)

        def z_out(j):
            each(nz - 1, lambda d: z_one(j, d).start())

        def z_one(j, d):
            k = lax.rem(zi + d, nz)
            return rc(buf(0, j, shard(k)), zr.at[j, zi], base[j] + 9 + k, zp(k), base[j] + 9 + nz + zi)

        def z_in(j):
            def one(d):
                z_one(j, d).wait_send()
                k = lax.rem(zi + d, nz)
                rc(zr.at[j, k], zr.at[j, k], base[j] + 9 + k, zp(k), base[j] + 9 + nz + k).wait_recv()

            each(nz - 1, one)

        def za_one(j, d):
            k = lax.rem(zi + d, nz)
            return rc(buf(0, j, shard(zi)), buf(0, j, shard(zi)), base[j] + 9 + 2 * nz + k, zp(k), base[j] + 9 + 3 * nz + zi)

        def za_in(j):
            def one(d):
                za_one(j, d).wait_send()
                k = lax.rem(zi + d, nz)
                rc(buf(0, j, shard(k)), buf(0, j, shard(k)), base[j] + 9 + 2 * nz + k, zp(k), base[j] + 9 + 3 * nz + k).wait_recv()

            each(nz - 1, one)

        def all_y(j):
            r = pl.ds(keep, q)
            return rc(buf(0, j, r), buf(0, j, r), base[j] + 5, Y)

        def all_c(j):
            r = pl.ds(mine, h)
            return rc(buf(0, j, r), buf(0, j, r), base[j] + 6, C)

        def free(j, i, dev):
            pl.semaphore_signal(ready.at[flag + 3 * j + i], inc=1, device_id=dev, device_id_type=MESH)

        def freed(j, i, k):
            pl.semaphore_wait(ready.at[flag + 3 * j + i], k)

        def cs(j, w):
            swap_c(j, w).start()

        def cd(j, w):
            swap_c(j, w).wait()
            if w == 0:
                free(j, 0, C)
            add_rows(h, buf(w, j, pl.ds(mine, h)), [co(j, w)])
            if not xs_first[j]:
                swap_y(j, w).start()
            elif w == 1:
                swap_x(j).start()

        def yd(j, w):
            swap_y(j, w).wait()
            if w == 0:
                free(j, 1, Y)
            add_rows(q, buf(w, j, pl.ds(keep, q)), [yr(j, w)])
            if xs_first[j]:
                z_out(j)
            elif w == 1:
                swap_x(j).start()

        def xd(j):
            swap_x(j).wait()
            if xs_first[j]:
                add_rows(h, buf(0, j, pl.ds(mine, h)), [xr(j)])
                swap_y(j, 0).start()
            else:
                add_rows(q, buf(0, j, pl.ds(keep, q)), [xr(j)])
                z_out(j)

        def zd(j):
            z_in(j)
            each(nz - 1, lambda d: free(j, 2, zp(lax.rem(zi + d, nz))))
            add_rows(s, buf(0, j, shard(zi)), [zr.at[j, lax.rem(zi + d, nz)] for d in range(1, nz)])
            for b, dev in enumerate(beyond):
                copy = rc(buf(0, j, shard(zi)), gr(j, b), base[j] + 9 + 4 * nz + b, dev)
                copy.start()
                copy.wait()
                add_rows(s, buf(0, j, shard(zi)), [gr(j, b)])
            freed(j, 2, nz - 1)
            each(nz - 1, lambda d: za_one(j, d).start())

        def zad(j):
            za_in(j)
            freed(j, 1, 1)
            all_y(j).start()

        def yad(j):
            all_y(j).wait()
            freed(j, 0, 1)
            all_c(j).start()

        def cad(j):
            all_c(j).wait()

        return dict(cs1=lambda j: cs(j, 1), cs0=lambda j: cs(j, 0), cd1=lambda j: cd(j, 1), cd0=lambda j: cd(j, 0),
                    yd1=lambda j: yd(j, 1), yd0=lambda j: yd(j, 0), xd=xd, zd=zd, zad=zad, yad=yad, cad=cad)

    ra = pa.shape[2]
    lanes = slice(0, WB)
    turns = [v for g in EVENTS.values() for v in g if v.endswith(".zd") and v[0] != "S"]
    slot = lambda name: turns.index(name) % 2
    set_a = make_set(NJ, ra, lambda w, j, r: pa.at[w, j, r], lambda j, w: ca.at[j, w],
                     lambda j: xa.at[j] if XA[j] else xa.at[j, 0 : ra // 4], lambda j, w: ya.at[j, 0] if w == 0 else xa.at[j, ra // 4 :], za, lambda j, b: ga.at[slot(f"A{j}.zd"), b], XA)
    oth_b = lambda j, r: pa.at[1, j % 2, r, pl.ds(al(j // 2 * WB, WB), WB)]
    buf_b = lambda w, j, r: oth_b(j, r) if w else pb.at[j, r]
    set_b = make_set(NJ, ra, buf_b, lambda j, w: ca.at[j, w, :, lanes],
                     lambda j: xb.at[j] if XB[j] else xb.at[j, 0 : ra // 4], lambda j, w: yb.at[j, 0] if w == 0 else xb.at[j, ra // 4 :], zb, lambda j, b: ga.at[slot(f"B{j}.zd"), b, :, lanes], XB)
    set_s = make_set(1, ps.shape[2], lambda w, j, r: ps.at[w, j, r], lambda j, w: cs.at[j, w],
                     lambda j: xs.at[j], lambda j, w: ys.at[j, w], zs, lambda j, b: gs.at[0, b], (False,))

    def out_a(j):
        own = pa.at[0, j]
        res = [(own.at[b * D : (b + 1) * D], gf.at[:, j * CH + b * WA : j * CH + (b + 1) * WA]) for b in range(CH // WA)]
        base = CH // WA * D
        res += [(own.at[base + b * CH : base + (b + 1) * CH], go.at[j * CH : (j + 1) * CH, b * WA : (b + 1) * WA])
                for b in range(D // WA)]
        return [pltpu.make_async_copy(u, v, ls.at[8 + j * 5 + i]) for i, (u, v) in enumerate(res)]

    def out_b(j):
        own = pb.at[j]
        res = [(own.at[t * D : (t + 1) * D], gq.at[t, :, j * WB : (j + 1) * WB]) for t in range(3)]
        res += [(own.at[3 * D + b * WB : 3 * D + (b + 1) * WB], gp.at[j * WB : (j + 1) * WB, b * WB : (b + 1) * WB])
                for b in range(D // WB)]
        return [pltpu.make_async_copy(u, v, ls.at[23 + j * 9 + i]) for i, (u, v) in enumerate(res)]

    def step(name):
        def run():
            where, stage = name.split(".")
            j = int(where[1:] or 0)
            {"A": set_a, "B": set_b, "S": set_s}[where[0]][stage](j)
            if stage == "cad":
                for c in {"A": out_a, "B": out_b, "S": out_s}[where[0]](j):
                    c.start()
        return run

    def out_s(j):
        return [pltpu.make_async_copy(ps.at[0, 0], sm, ls.at[54])]

    def do(names):
        for name in names:
            kind, _, rest = name.partition(".")
            if kind[0] == "W":
                wstep(int(kind[1:]), int(rest[1:]))
            elif kind[:3] == "out":
                out_copy[int(kind[3:])].start()
            elif kind[:3] == "gin":
                gin_copy[int(kind[3:])].start()
            else:
                step(name)()

    def ticks(where, t):
        for g, name in enumerate(where):
            if EVENTS.get(name):
                @pl.when(t == g)
                def _(name=name):
                    do(EVENTS[name])

    def put(i, v):
        for w in (0, 1):
            for b in range(D // 128):
                ps[w, 0, i * 8 + b : i * 8 + b + 1, :] = v[:, b * 128 : (b + 1) * 128]

    ps[...] = jnp.zeros_like(ps)

    wstep(0, 0)
    wstep(0, 1)
    def ln_row(r, _):
        rr = rows_of(r)
        n1, _inv = norm(xf[rr, :].astype(F))
        a = (n1 * g1[...] + s1[...]).astype(B)
        a2[rr, :] = a
        a1t[:, rr] = a.T
        return 0

    local[0].wait()
    own_rows = ti * (T // RT // 2)
    lax.fori_loop(own_rows, own_rows + T // RT // 2, ln_row, 0)
    wstep(0, 2)
    x_copy.wait()
    wsend(4, 0)
    wsend(1, 0)
    bf_copy.start()
    wsend(2, 0)
    c_copy.start()
    wsend(3, 0)

    lax.fori_loop(T // RT // 2 - own_rows, T // RT - own_rows, ln_row, 0)
    bq_copy.wait()
    for c in local[3:]:
        c.wait()
    wstep(0, 3)
    do(EVENTS["ln"])

    def qkv_row(r, _):
        rr = rows_of(r)
        a = a2[rr, :]
        for t in range(3):
            v = nn(a, wqkv[:, t * D : (t + 1) * D])
            for k, b in enumerate((bq, bqo)):
                u = v[:, k * HW : (k + 1) * HW]
                if t != 1:
                    u = u + b[t // 2 : t // 2 + 1, :]
                if t == 0:
                    u = u * 0.125
                qkv[rr, t * D + k * HW : t * D + (k + 1) * HW] = u.astype(B)
        ticks(["q0", "q1", "q2", "q3"], r)
        return 0

    lax.fori_loop(0, T // RT, qkv_row, 0)

    def fwd(hp, _):
        pair_attention(hp, n, qkv, o, lse)
        ticks([f"f{i}" for i in range(6)], hp)
        return 0

    lax.fori_loop(0, NP, fwd, 0)
    local[1].wait()
    local[2].wait()
    do(EVENTS["mid0"])
    c_copy.wait()
    bf_copy.wait()

    def fetch(which, j):
        cols = pl.ds(al(j * CH, CH), CH)
        s1 = (wf if which == 0 else lf).at[:, cols]
        s2 = (wo if which == 0 else lo).at[cols, :]
        return [pltpu.make_async_copy(s1, wb1.at[which], ls.at[50 + which]),
                pltpu.make_async_copy(s2, wb2.at[which], ls.at[52 + which])]

    phase_mid(n, xf, cf, o, wproj, bproj, g2, s2, r1, a2, dm, put)
    m[...] = jnp.zeros_like(m)
    da2[...] = jnp.zeros_like(da2)
    do(EVENTS["mid1"])
    do(EVENTS["mid2"])
    for c in fetch(1, 0):
        c.start()

    def chunk(t, _):
        which = 1 - lax.rem(t, 2)
        j = t // 2
        for w in (0, 1):
            @pl.when(which == w)
            def _(w=w):
                for c in fetch(w, j):
                    c.wait()

        bias = jnp.where(which == 0, bfm[pl.ds(j, 1), :], bfo[pl.ds(j, 1), :])
        tot = mlp_rows(wb1.at[which], wb2.at[which], bias, a2, dm, m, da2, hd)
        for b in range(CH // 128):
            ps[which, 0, pl.ds(64 + j * 4 + b, 1), :] = tot[:, b * 128 : (b + 1) * 128]
        ticks([f"m{i}a" for i in range(6)], t)
        for w in (0, 1):
            @pl.when((which == 1 - w) & (t < 5))
            def _(w=w):
                for c in fetch(w, (t + 1) // 2):
                    c.start()
        mlp_grads(a2, dm, hd, pa.at[which, j])
        ticks([f"m{i}b" for i in range(6)], t)
        return 0

    lax.fori_loop(0, 6, chunk, 0)

    phase_back(n, cf, r1, m, da2, bout, g2, wproj, dm, hd, a2, put)
    out_own = pltpu.make_async_copy(a2.at[half(ti)], out.at[ti], ls.at[6])
    gin_own = pltpu.make_async_copy(dm.at[half(ti)], gin.at[ti], ls.at[7])
    out_own.start()
    do(EVENTS["back"])

    def bwd(t, _):
        which, j = (1 - t // NJ, lax.rem(t, NJ)) if ORDER == "oth" else (1 - lax.rem(t, 2), t // 2)
        hp = which * NJ + j
        pair_backward(hp, n, qkv, hd, o, lse, m)
        ticks([f"b{i}a" for i in range(6)], t)
        off = al(hp * 128, 128)
        d = jnp.concatenate([qkv[:, pl.ds(k * D + off, 128)] for k in range(3)], axis=1)
        g = nn(a1t[...], d).astype(B)
        e = tn(o[:, pl.ds(off, 128)], dm[...]).astype(B)

        def store(piece):
            for k in range(3):
                piece[k * D : (k + 1) * D, :] = g[:, k * 128 : (k + 1) * 128]
            for b in range(D // WB):
                piece[3 * D + b * WB : 3 * D + (b + 1) * WB, :] = e[:, b * WB : (b + 1) * WB]

        @pl.when(which == 0)
        def _():
            store(pb.at[j])

        @pl.when(which == 1)
        def _():
            store(oth_b(j, slice(None)))

        for k, base in ((0, 48), (2, 56)):
            v = jnp.sum(qkv[:, pl.ds(k * D + off, 128)].astype(F), axis=0, keepdims=True)
            ps[which, 0, pl.ds(base + j, 1), :] = v
        ticks([f"b{i}b" for i in range(6)], t)
        return 0

    lax.fori_loop(0, 6, bwd, 0)
    first = (T // RT // 2) * (1 - ti)
    sums = phase_end(xf, qkv, wqkv, g1, da2, dm, first, None)
    do(EVENTS["end1"])
    do(EVENTS["end1b"])
    a, b = phase_end(xf, qkv, wqkv, g1, da2, dm, T // RT // 2 - first, sums)
    put(0, a)
    put(1, b)
    gin_own.start()
    do(EVENTS["end2"])
    do(EVENTS["drain"])
    for j in range(NJ):
        for c in out_a(j) + out_b(j):
            c.wait()
    for c in out_s(0) + [out_own, gin_own] + out_copy + gin_copy:
        c.wait()
    assert count[0] <= SEMS(dp)


def SEMS(dp):
    return 64 + 7 * (25 + depth(dp))


def local_call(dp, *args):
    V = pl.BlockSpec(memory_space=pltpu.VMEM)
    S = pl.BlockSpec(memory_space=pltpu.SMEM)
    A = pl.BlockSpec(memory_space=pl.ANY)
    sd = jax.ShapeDtypeStruct
    ra, rsm, nz = 4 * D, 256, 4
    nb = max(depth(dp), 1)
    outs = (sd((2, T // 2, D), B), sd((2, T // 2, D), B), sd((3, D, HW), B), sd((HW, D), B), sd((D, FH), B),
            sd((FH, D), B), sd((rsm, 128), F), sd((D, FH), B), sd((FH, D), B))
    vm = pltpu.VMEM
    sem = pltpu.SemaphoreType.DMA

    def buffers(k, r, w, x_first, dt):
        return [vm((2, k, r, w), dt), vm((k, 2, r // 2, w), dt), vm((k, r // 2 if x_first else r // 4, w), dt),
                vm((k, 1 if x_first else 2, r // 4, w), dt), vm((k, nz, r // 4 // nz, w), dt), vm((min(k, 2), nb, r // 4 // nz, w) if dp > 16 else (1, 1, 16, 128), dt)]

    return pl.pallas_call(
        functools.partial(kernel, dp),
        out_shape=outs,
        in_specs=[S, A, A, A, V, A, A, A] + [V] * 7,
        out_specs=(A,) * 9,
        scratch_shapes=[
            vm((T, D), B), vm((T, D), B), vm((D, T), B), vm((D, 3 * D), B), vm((D, D), B), vm((2, HW), F), vm((8, CH), F), vm((8, CH), F),
            vm((2, D, CH), B), vm((2, CH, D), B), vm((T, 3 * D), B), vm((T, D), B), vm((16, T), F), vm((T, D), F),
            vm((T, D), B), vm((T, D), B), vm((T, D), F), vm((T, D), F), vm((T, 2 * CH), B),
        ] + buffers(NJ, ra, WA, True, B) + [vm((NJ, ra, WB), B)] + buffers(NJ, ra, WB, True, B)[2:5] + buffers(1, rsm, 128, False, F)
        + [sem((SEMS(dp),)), sem((SEMS(dp),)), sem((56,)), pltpu.SemaphoreType.REGULAR((21,))],
        compiler_params=pltpu.CompilerParams(vmem_limit_bytes=VLIMIT, collective_id=0, has_side_effects=True),
    )(*args)


VLIMIT = 63 * 2**20 + 2**19


def body(dp, inputs, cotangent, lengths, gain_one, shift_one, qkv_weight, qv_bias, proj_weight, proj_bias, gain_two,
         shift_two, fc_weight, fc_bias, out_weight, out_bias):
    res = local_call(
        dp, lengths.reshape(1, 2), inputs.reshape(2, T // 2, D), cotangent.reshape(2, T // 2, D),
        jnp.transpose(qkv_weight, (1, 0, 2)), qv_bias, proj_weight, fc_weight, out_weight, gain_one, shift_one,
        proj_bias, gain_two, shift_two, out_bias, fc_bias)
    out, gin, gq, gp, gf, go, gqv, gfb, *vec = widen(*res[:7])
    rows = lambda v: v[:, None]
    return (rows(out), rows(gin), vec[0], vec[1], jnp.transpose(gq, (1, 0, 2)), gqv, gp, vec[2], vec[3], vec[4], gf, gfb,
            go, vec[5])


def widen_kernel(*refs):
    srcs, sm, dsts, (gqv, gfb, *vec), (ins, outs, si, so) = refs[:6], refs[6], refs[7:13], refs[13:21], refs[21:]
    tiles = []
    for s, d in zip(srcs, dsts):
        for a in range(s.shape[0] if len(s.shape) == 3 else 1):
            u, v = (s.at[a], d.at[a]) if len(s.shape) == 3 else (s, d)
            step = min(512, u.shape[0])
            for b in range(0, u.shape[0], step):
                tiles.append((u.at[b : b + step], v.at[b : b + step], u.shape[1], min(step, u.shape[0] - b)))
    place, row, col = [], 0, 0
    for _u, _v, wide, n in tiles:
        if col + wide > FH:
            row, col = row + 1, 0
        place.append((row, pl.ds(0, n), pl.ds(col, wide)))
        col += wide
    def load(i):
        r, a, b = place[i]
        return pltpu.make_async_copy(tiles[i][0], ins.at[r, a, b], si.at[i])
    def save(i):
        r, a, b = place[i]
        return pltpu.make_async_copy(outs.at[r, a, b], tiles[i][1], so.at[i])
    for i in range(len(tiles)):
        load(i).start()
    for i in range(6):
        for b in range(D // 128):
            vec[i][b * 128 : (b + 1) * 128] = sm[i * 8 + b, :]
    for b in range(FH // 128):
        gfb[b * 128 : (b + 1) * 128] = sm[64 + b, :]
    for b in range(HW // 128):
        gqv[0:1, b * 128 : (b + 1) * 128] = sm[48 + b : 49 + b, :]
        gqv[1:2, b * 128 : (b + 1) * 128] = sm[56 + b : 57 + b, :]
    for i in range(len(tiles)):
        load(i).wait()
        r, _a, b = place[i]
        n = tiles[i][3]

        def step(k, _):
            rr = pl.ds(pl.multiple_of(k * 64, 64), 64)
            outs[r, rr, b] = ins[r, rr, b].astype(F)
            return 0

        lax.fori_loop(0, n // 64, step, 0)
        save(i).start()
    for i in range(len(tiles)):
        save(i).wait()


def widen(*args):
    V = pl.BlockSpec(memory_space=pltpu.VMEM)
    A = pl.BlockSpec(memory_space=pl.ANY)
    sd = jax.ShapeDtypeStruct
    wide = [sd(v.shape, F) for v in args[:6]]
    small = [sd((2, HW), F), sd((FH,), F)] + [sd((D,), F)] * 6
    sem = pltpu.SemaphoreType.DMA
    return pl.pallas_call(
        widen_kernel,
        out_shape=tuple(wide + small),
        in_specs=[A] * 6 + [V],
        out_specs=tuple([A] * 6 + [V] * 8),
        scratch_shapes=[pltpu.VMEM((9, 512, FH), B), pltpu.VMEM((9, 512, FH), F), sem((24,)), sem((24,))],
        compiler_params=pltpu.CompilerParams(vmem_limit_bytes=56 * 2**20),
    )(*args)


def solution(mesh):
    dp = P(None, "dp", "tensor", None)
    return jax.shard_map(
        functools.partial(body, mesh.shape["dp"]),
        mesh=mesh,
        in_specs=(dp, dp, P(None, "dp"), P(), P(), P(None, None, "tensor"), P(None, "tensor"), P("tensor", None), P(),
                  P(), P(), P(None, "tensor"), P("tensor"), P("tensor", None), P()),
        out_specs=(dp, dp, P(), P(), P(None, None, "tensor"), P(None, "tensor"), P("tensor", None), P(), P(), P(),
                   P(None, "tensor"), P("tensor"), P("tensor", None), P()),
        check_vma=False,
    )
```

```python
import functools

import jax
import jax.numpy as jnp
from jax import lax
from jax.experimental import pallas as pl
from jax.experimental.pallas import tpu as pltpu
from jax.sharding import PartitionSpec as P

F = jnp.float32
B = jnp.bfloat16
T = 1024
D = 768
HD = 64
HW = 384
FF = 3072
FH = 1536
CH = 512
RT = 256
QB = 256
NP = 6
EPS = 1e-05
SB = 48 ** (-0.5)
RC = 0.7978845608028654
CC = 0.044715


def nn(a, b):
    return lax.dot_general(a, b, (((1,), (0,)), ((), ())), preferred_element_type=F)


def nt(a, b):
    return lax.dot_general(a, b, (((1,), (1,)), ((), ())), preferred_element_type=F)


def tn(a, b):
    return lax.dot_general(a, b, (((0,), (0,)), ((), ())), preferred_element_type=F)


def rows_of(r):
    return pl.ds(pl.multiple_of(r * RT, RT), RT)


def norm(v):
    cen = v - jnp.mean(v, axis=-1, keepdims=True)
    inv = lax.rsqrt(jnp.mean(cen * cen, axis=-1, keepdims=True) + EPS)
    return cen * inv, inv


def norm_back(e, n, inv):
    return inv * (e - jnp.mean(e, axis=-1, keepdims=True) - n * jnp.mean(e * n, axis=-1, keepdims=True))


def gelu_pair(u):
    u2 = u * u
    t = jnp.tanh(RC * (u + CC * u2 * u))
    hp = 0.5 * (1.0 + t)
    return u * hp, hp + (0.5 * RC) * u * (1.0 - t * t) * (1.0 + (3.0 * CC) * u2)


def pair_attention(hp, n, qkv, o, lse):
    off = pl.multiple_of(hp * 128, 128)
    lane = lax.broadcasted_iota(jnp.int32, (QB, 128), 1)
    for qb in range(T // QB):
        ext = (qb + 1) * QB
        q2 = qkv[pl.ds(qb * QB, QB), pl.ds(off, 128)]
        k2 = qkv[pl.ds(0, ext), pl.ds(D + off, 128)]
        v2 = qkv[pl.ds(0, ext), pl.ds(2 * D + off, 128)]
        key = lax.broadcasted_iota(jnp.int32, (ext, QB), 0)
        qi = lax.broadcasted_iota(jnp.int32, (ext, QB), 1) + qb * QB
        bound = jnp.minimum(qi + 1, n)
        outs = []
        for h in range(2):
            qm = jnp.where((lane // HD) == h, q2, jnp.zeros_like(q2))
            s = jnp.where(key < bound, nt(k2, qm), -1e30)
            m = jnp.max(s, axis=0, keepdims=True)
            e = jnp.exp(s - m)
            l = jnp.sum(e, axis=0, keepdims=True)
            pb = (e * (1.0 / l)).astype(B)
            outs.append(tn(pb, v2))
            lse[pl.ds(hp * 2 + h, 1), pl.ds(qb * QB, QB)] = m + jnp.log(l)
        o[pl.ds(qb * QB, QB), pl.ds(off, 128)] = jnp.where(lane < HD, outs[0], outs[1]).astype(B)


def pair_backward(hp, n, qkv, do, o, lse, acc):
    off = pl.multiple_of(hp * 128, 128)
    lane = lax.broadcasted_iota(jnp.int32, (QB, 128), 1)
    for qb in reversed(range(T // QB)):
        ext = (qb + 1) * QB
        rq = pl.ds(qb * QB, QB)
        q2 = qkv[rq, pl.ds(off, 128)]
        k2 = qkv[pl.ds(0, ext), pl.ds(D + off, 128)]
        v2 = qkv[pl.ds(0, ext), pl.ds(2 * D + off, 128)]
        do2 = do[rq, pl.ds(off, 128)]
        o2 = o[rq, pl.ds(off, 128)]
        prod = (do2.astype(F) * o2.astype(F)).T
        key = lax.broadcasted_iota(jnp.int32, (ext, QB), 0)
        qi = lax.broadcasted_iota(jnp.int32, (ext, QB), 1) + qb * QB
        bound = jnp.minimum(qi + 1, n)
        dqs, dks, dvs = [], [], []
        for h in range(2):
            hm = (lane // HD) == h
            qm = jnp.where(hm, q2, jnp.zeros_like(q2))
            dm = jnp.where(hm, do2, jnp.zeros_like(do2))
            dd = jnp.sum(prod[h * HD : (h + 1) * HD], axis=0, keepdims=True)
            ls = lse[pl.ds(hp * 2 + h, 1), rq]
            p = jnp.where(key < bound, jnp.exp(nt(k2, qm) - ls), 0.0)
            ds = (p * (nt(v2, dm) - dd)).astype(B)
            dqs.append(tn(k2, ds).T)
            dks.append(nn(ds, qm))
            dvs.append(nn(p.astype(B), dm))
        qkv[rq, pl.ds(off, 128)] = (jnp.where(lane < HD, dqs[0], dqs[1]) * 0.125).astype(B)
        dk = dks[0] + dks[1]
        dv = dvs[0] + dvs[1]
        if qb == T // QB - 1:
            acc[:, 0:128] = dk
            acc[:, 128:256] = dv
        else:
            acc[pl.ds(0, ext), 0:128] += dk
            acc[pl.ds(0, ext), 128:256] += dv
    qkv[:, pl.ds(D + off, 128)] = acc[:, 0:128].astype(B)
    qkv[:, pl.ds(2 * D + off, 128)] = acc[:, 128:256].astype(B)


def phase_mid(x, o, wproj, bproj, g2, s2, r1, a2):
    def row(r, _):
        rr = rows_of(r)
        v = x[rr, :].astype(F) + SB * (nn(o[rr, :], wproj[...]) + bproj[...])
        r1[rr, :] = v
        n2, _inv = norm(v)
        a2[rr, :] = (n2 * g2[...] + s2[...]).astype(B)
        return 0

    lax.fori_loop(0, T // RT, row, 0)


def phase_cot(n, c, dm):
    def row(r, ob):
        rr = rows_of(r)
        ids = lax.broadcasted_iota(jnp.int32, (RT, 1), 0) + r * RT
        cs = SB * (c[rr, :].astype(F) * (ids < n).astype(F))
        dm[rr, :] = cs.astype(B)
        return ob + jnp.sum(cs, axis=0, keepdims=True)

    return lax.fori_loop(0, T // RT, row, jnp.zeros((1, D), F))


def phase_back(n, c, r1, m, da2, bout, g2, wproj, dattn, do, out, put):
    def row(r, acc):
        rr = rows_of(r)
        v = r1[rr, :]
        out[rr, :] = (v + SB * (m[rr, :] + bout[...])).astype(B)
        n2, inv = norm(v)
        g = da2[rr, :]
        ids = lax.broadcasted_iota(jnp.int32, (RT, 1), 0) + r * RT
        dr = c[rr, :].astype(F) * (ids < n).astype(F) + norm_back(g * g2[...], n2, inv)
        da2[rr, :] = dr
        sr = SB * dr
        sb = sr.astype(B)
        dattn[rr, :] = sb
        do[rr, 0:D] = nt(sb, wproj[...]).astype(B)
        total = lambda w: jnp.sum(w, axis=0, keepdims=True)
        return acc[0] + total(g * n2), acc[1] + total(g), acc[2] + total(sr)

    z = jnp.zeros((1, D), F)
    a, b, p = lax.fori_loop(0, T // RT, row, (z, z, z))
    put(2, p)
    put(3, a)
    put(4, b)


def phase_end(x, qkv, wqkv, g1, dr1, gin, first, sums):
    def row(r, acc):
        rr = rows_of(r)
        g = nt(qkv[rr, :], wqkv[...])
        n1, inv = norm(x[rr, :].astype(F))
        gin[rr, :] = (dr1[rr, :] + norm_back(g * g1[...], n1, inv)).astype(B)
        total = lambda w: jnp.sum(w, axis=0, keepdims=True)
        return acc[0] + total(g * n1), acc[1] + total(g)

    z = jnp.zeros((1, D), F)
    return lax.fori_loop(first, first + T // RT // 2, row, (z, z) if sums is None else sums)


EVENTS = {
    "ln": (),
    "q0": (),
    "q1": (),
    "q2": (),
    "q3": ("W1.w0",),
    "f0": ("W4.w0",),
    "f1": ("W2.w0", "W1.w1",),
    "f2": ("W3.w0", "W4.w1",),
    "f3": ("W2.w1",),
    "f4": ("W4.w2",),
    "f5": ("W1.w2", "W4.w3",),
    "mid0": (),
    "mid1": ("W2.w2",),
    "mid2": ("W1.w3",),
    "m0a": ("W3.w1", "W2.w3",),
    "m0b": ("A0.cs1",),
    "m1a": (),
    "m1b": ("A0.cs0", "A0.cd1",),
    "m2a": ("W3.w2",),
    "m2b": ("A1.cs1", "A0.cd0",),
    "m3a": ("W3.w3", "A0.yd1",),
    "m3b": ("A1.cs0", "A1.cd1",),
    "m4a": ("A1.cd0", "A0.yd0",),
    "m4b": ("A2.cs1", "A0.xd",),
    "m5a": (),
    "m5b": ("A2.cs0", "A2.cd1", "A1.yd1",),
    "back": ("A2.cd0", "A0.zd",),
    "proj": ("P.cs1", "P.cs0",),
    "b0a": ("out0", "A1.yd0", "A1.xd", "P.cd1", "P.cd0",),
    "b0b": ("B0.cs1",),
    "b1a": ("A2.yd1", "A0.zad",),
    "b1b": ("B1.cs1",),
    "b2a": ("A2.yd0", "A1.zd", "B0.cd1", "P.xd", "B1.cd1",),
    "b2b": ("B2.cs1",),
    "b3a": ("B2.cd1",),
    "b3b": ("B0.cs0", "A2.xd", "A0.yad",),
    "b4a": ("B0.cd0", "P.yd0", "A1.zad",),
    "b4b": ("B1.cs0", "A0.cad",),
    "b5a": ("A2.zd", "B1.cd0", "B0.xd", "B1.xd",),
    "b5b": ("B2.cs0", "A1.yad", "out1", "B2.cd0", "P.zd",),
    "end1": ("B2.xd", "out2", "B0.yd0",),
    "end1b": (),
    "end2": ("S.cs1", "S.cs0", "A1.cad", "B1.yd0",),
    "drain": ("A2.zad", "out3", "S.cd1", "P.zad", "B2.yd0", "S.cd0", "B0.zd", "gin0", "B1.zd", "gin1", "A2.yad",
        "S.yd1", "B2.zd", "P.yad", "gin2", "B0.zad", "S.yd0", "A2.cad", "S.xd", "B1.zad", "P.cad", "gin3",
        "B0.yad", "B2.zad", "S.zd", "B1.yad", "B0.cad", "S.zad", "B2.yad", "B1.cad", "S.yad", "B2.cad", "S.cad",),
}
WAY = ("zy", "zy", "yz", "yz", "yz")
XA = (False, False, False)
XB = (True, True, True)
XP = (True,)
FIRST = "oth"
AFTER = (1, 4, 2, 3, 0)
COUNT = 4
ORDER = "oth"
MESH = pl.DeviceIdType.MESH
NJ = 3
WA = 256
WB = 128


def each(n, fn):
    if n <= 3:
        for d in range(1, n + 1):
            fn(d)
    else:
        lax.fori_loop(1, n + 1, lambda d, _: (fn(d), 0)[1], 0)


def add_rows(rows, dst, srcs):
    step = next(s for s in (192, 128, 64, 32, 16) if rows % s == 0)

    def tile(i, _):
        rr = pl.ds(pl.multiple_of(i * step, step), step)
        v = dst[rr, :].astype(F)
        for s in srcs:
            v = v + s[rr, :].astype(F)
        dst[rr, :] = v.astype(dst.dtype)
        return 0

    lax.fori_loop(0, rows // step, tile, 0)


def depth(dp):
    return (dp // 16 - 1).bit_length()


def mlp_rows(w1, w2, bias, a2, dm, m, da2, hd):
    tot = jnp.zeros((1, CH), F)
    for r in range(T // RT):
        rr = pl.ds(r * RT, RT)
        u = nn(a2[rr, :], w1[...]) + bias
        h, sl = gelu_pair(u)
        hb = h.astype(B)
        hd[rr, 0:CH] = hb
        du = (nt(dm[rr, :], w2[...]) * sl).astype(B)
        hd[rr, CH : 2 * CH] = du
        m[rr, :] += nn(hb, w2[...])
        da2[rr, :] += nt(du, w1[...])
        tot = tot + jnp.sum(du.astype(F), axis=0, keepdims=True)
    return tot


def mlp_grads(a2, dm, hd, piece):
    for k in range(D // 256):
        g = tn(a2[:, k * 256 : (k + 1) * 256], hd[:, CH : 2 * CH]).astype(B)
        for b in range(CH // WA):
            piece[b * D + k * 256 : b * D + (k + 1) * 256, :] = g[:, b * WA : (b + 1) * WA]
    base = CH // WA * D
    for k in range(CH // 256):
        g = tn(hd[:, k * 256 : (k + 1) * 256], dm[...]).astype(B)
        for b in range(D // WA):
            piece[base + b * CH + k * 256 : base + b * CH + (k + 1) * 256, :] = g[:, b * WA : (b + 1) * WA]


class Row:
    def __init__(self, ref):
        self.ref = ref

    def __getitem__(self, _):
        return self.ref[...].reshape(1, -1)


def kernel(dp, lens, inp, cot, wq, bq, wp, wf, wo, g1, s1, bproj, g2, s2, bout, fcb,
           out, gin, gq, gp, gf, go, sm, lf, lo,
           xf, cf, a1t, wqkv, wproj, bqo, bfm, bfo, wb1, wb2, qkv, o, lse, r1, a2, dm, m, da2, hd,
           pa, ca, xa, ya, za, ga, pb, xb, yb, zb, pp, op, cp, xp, yp, zp_, ps, cs, xs, ys, zs, gs, ss, rs, ls, ready):
    g1, s1, bproj, g2, s2, bout = (Row(v) for v in (g1, s1, bproj, g2, s2, bout))
    ti = lax.axis_index("tensor")
    me = lax.axis_index("dp")
    nz = 4
    cc = lax.rem(me, 2)
    yy = lax.rem(me // 2, 2)
    zi = lax.rem(me // 4, nz)
    beyond = [{"dp": me + (1 - 2 * lax.rem(me // (16 << b), 2)) * (16 << b)} for b in range(depth(dp))]
    z1 = lax.rem(zi, 2)
    X = {"tensor": 1 - ti}
    C = {"dp": me + 1 - 2 * cc}
    Y = {"dp": me + 2 - 4 * yy}
    Z1 = {"dp": me + 4 - 8 * z1}
    zp = lambda k: {"dp": me + (k - zi) * 4}
    al = pl.multiple_of
    count = [0]
    flags = [0]

    def new(k=1):
        count[0] += k
        return count[0] - k

    def rc(src, dst, i, dev, j=None):
        return pltpu.make_async_remote_copy(src_ref=src, dst_ref=dst, send_sem=ss.at[i], recv_sem=rs.at[i if j is None else j],
                                            device_id=dev, device_id_type=MESH)

    bar = pltpu.get_barrier_semaphore()
    for dev in (X, C, Y):
        pl.semaphore_signal(bar, inc=1, device_id=dev, device_id_type=MESH)
    each(nz - 1, lambda d: pl.semaphore_signal(bar, inc=1, device_id=zp(lax.rem(zi + d, nz)), device_id_type=MESH))
    for dev in beyond:
        pl.semaphore_signal(bar, inc=1, device_id=dev, device_id_type=MESH)
    pl.semaphore_wait(bar, 3 + nz - 1 + len(beyond))

    def units(group):
        if group == 0:
            return [(wq.at[t], lambda r, t=t: wqkv.at[r, t * D + HW : (t + 1) * D], D) for t in range(3)]
        if group == 4:
            return [(wp, lambda r: wproj.at[pl.ds(al(HW + r.start, 16), r.size), :], HW)]
        j = group - 1
        cols = slice(j * CH, (j + 1) * CH)
        return [(wf.at[:, cols], lambda r: lf.at[r, cols], D),
                (wo.at[cols, :], lambda r: lo.at[pl.ds(al(j * CH + r.start, 16), r.size), :], CH)]

    wsem = [new(4 * len(units(g))) for g in range(5)]

    def wcopies(group, stage):
        res = []
        first, second = ((z1, Z1), (yy, Y))[:: 1 if WAY[group] == "zy" else -1]
        for i, (own, land, n) in enumerate(units(group)):
            e = n // 8
            if stage < 2:
                r = pl.ds(al((cc * 4 + second[0] * 2 + first[0]) * e, 16), e)
            elif stage == 2:
                r = pl.ds(al((cc * 2 + second[0]) * 2 * e, 16), 2 * e)
            else:
                r = pl.ds(al(cc * 4 * e, 16), 4 * e)
            src = own.at[r, :] if stage == 0 else land(r)
            dev = (X, first[1], second[1], C)[stage]
            res.append(rc(src, land(r), wsem[group] + stage * len(units(group)) + i, dev))
        return res

    def wsend(group, stage):
        for c in wcopies(group, stage):
            c.start()

    def wstep(group, stage):
        nexts = wcopies(group, stage + 1) if stage < 3 else [None] * len(units(group))
        for c, d in zip(wcopies(group, stage), nexts):
            c.wait()
            if d is not None:
                d.start()

    half = lambda i: pl.ds(al(i * (T // 2), T // 2), T // 2)
    si = new(12)
    x_copy = rc(inp.at[1 - ti], xf.at[half(ti)], si, X)
    c_copy = rc(cot.at[1 - ti], cf.at[half(ti)], si + 1, X)
    bq_copy = rc(bq, bqo, si + 2, X)
    bf_copy = rc(bfm, bfo, si + 3, X)
    def rows_back(v, res, i):
        q = T // 2 // COUNT
        there = lambda b, k: pl.ds(al(b * (T // 2) + k * q, 16), q)
        return [rc(v.at[there(1 - ti, k)], res.at[ti, k * q : (k + 1) * q], si + i + k, X) for k in range(COUNT)]

    out_copy = rows_back(a2, out, 4)
    gin_copy = rows_back(dm, gin, 8)
    local = [pltpu.make_async_copy(inp.at[ti], xf.at[half(ti)], ls.at[0]),
             pltpu.make_async_copy(cot.at[ti], cf.at[half(ti)], ls.at[1]),
             pltpu.make_async_copy(wp, wproj.at[0:HW], ls.at[2])]
    local += [pltpu.make_async_copy(wq.at[t], wqkv.at[:, t * D : t * D + HW], ls.at[3 + t]) for t in range(3)]
    wsend(0, 0)
    bq_copy.start()
    x_copy.start()
    for c in local:
        c.start()

    n = lens[0, ti]
    for j in range(NJ):
        bfm[j : j + 1, :] = fcb[j * CH : (j + 1) * CH].reshape(1, CH)
    bfm[NJ:, :] = jnp.zeros((8 - NJ, CH), F)

    def make_set(k_pieces, rows, buf, co, xr, yr, zr, gr, xs_first):
        h, q = rows // 2, rows // 4
        s = q // nz
        base = [new(9 + 4 * nz + len(beyond)) for _ in range(k_pieces)]
        flag = flags[0]
        flags[0] += 3 * k_pieces
        mine = al(cc * h, 16)
        keep = al(cc * h + yy * q, 16)
        give = al(cc * h + (1 - yy) * q, 16)
        shard = lambda k: pl.ds(al(keep + k * s, 8), s)

        def swap_c(j, w):
            return rc(buf(w, j, pl.ds(al((1 - cc) * h, 16), h)), co(j, w), base[j] + w, C)

        def swap_x(j):
            src = buf(1, j, pl.ds(mine, h)) if xs_first[j] else buf(1, j, pl.ds(keep, q))
            return rc(src, xr(j), base[j] + 2, X)

        def swap_y(j, w):
            return rc(buf(w, j, pl.ds(give, q)), yr(j, w), base[j] + 3 + w, Y)

        def z_out(j):
            each(nz - 1, lambda d: z_one(j, d).start())

        def z_one(j, d):
            k = lax.rem(zi + d, nz)
            return rc(buf(0, j, shard(k)), zr(j, zi), base[j] + 9 + k, zp(k), base[j] + 9 + nz + zi)

        def z_in(j):
            def one(d):
                z_one(j, d).wait_send()
                k = lax.rem(zi + d, nz)
                rc(zr(j, k), zr(j, k), base[j] + 9 + k, zp(k), base[j] + 9 + nz + k).wait_recv()

            each(nz - 1, one)

        def za_one(j, d):
            k = lax.rem(zi + d, nz)
            return rc(buf(0, j, shard(zi)), buf(0, j, shard(zi)), base[j] + 9 + 2 * nz + k, zp(k), base[j] + 9 + 3 * nz + zi)

        def za_in(j):
            def one(d):
                za_one(j, d).wait_send()
                k = lax.rem(zi + d, nz)
                rc(buf(0, j, shard(k)), buf(0, j, shard(k)), base[j] + 9 + 2 * nz + k, zp(k), base[j] + 9 + 3 * nz + k).wait_recv()

            each(nz - 1, one)

        def all_y(j):
            r = pl.ds(keep, q)
            return rc(buf(0, j, r), buf(0, j, r), base[j] + 5, Y)

        def all_c(j):
            r = pl.ds(mine, h)
            return rc(buf(0, j, r), buf(0, j, r), base[j] + 6, C)

        def free(j, i, dev):
            pl.semaphore_signal(ready.at[flag + 3 * j + i], inc=1, device_id=dev, device_id_type=MESH)

        def freed(j, i, k):
            pl.semaphore_wait(ready.at[flag + 3 * j + i], k)

        def cs(j, w):
            swap_c(j, w).start()

        def cd(j, w):
            swap_c(j, w).wait()
            if w == 0:
                free(j, 0, C)
            add_rows(h, buf(w, j, pl.ds(mine, h)), [co(j, w)])
            if not xs_first[j]:
                swap_y(j, w).start()
            elif w == 1:
                swap_x(j).start()

        def yd(j, w):
            swap_y(j, w).wait()
            if w == 0:
                free(j, 1, Y)
            add_rows(q, buf(w, j, pl.ds(keep, q)), [yr(j, w)])
            if xs_first[j]:
                z_out(j)
            elif w == 1:
                swap_x(j).start()

        def xd(j):
            swap_x(j).wait()
            if xs_first[j]:
                add_rows(h, buf(0, j, pl.ds(mine, h)), [xr(j)])
                swap_y(j, 0).start()
            else:
                add_rows(q, buf(0, j, pl.ds(keep, q)), [xr(j)])
                z_out(j)

        def zd(j):
            z_in(j)
            each(nz - 1, lambda d: free(j, 2, zp(lax.rem(zi + d, nz))))
            add_rows(s, buf(0, j, shard(zi)), [zr(j, lax.rem(zi + d, nz)) for d in range(1, nz)])
            for b, dev in enumerate(beyond):
                copy = rc(buf(0, j, shard(zi)), gr(j, b), base[j] + 9 + 4 * nz + b, dev)
                copy.start()
                copy.wait()
                add_rows(s, buf(0, j, shard(zi)), [gr(j, b)])
            freed(j, 2, nz - 1)
            each(nz - 1, lambda d: za_one(j, d).start())

        def zad(j):
            za_in(j)
            freed(j, 1, 1)
            all_y(j).start()

        def yad(j):
            all_y(j).wait()
            freed(j, 0, 1)
            all_c(j).start()

        def cad(j):
            all_c(j).wait()

        return dict(cs1=lambda j: cs(j, 1), cs0=lambda j: cs(j, 0), cd1=lambda j: cd(j, 1), cd0=lambda j: cd(j, 0),
                    yd1=lambda j: yd(j, 1), yd0=lambda j: yd(j, 0), xd=xd, zd=zd, zad=zad, yad=yad, cad=cad)

    ra = pa.shape[2]
    lanes = slice(0, WB)
    turns = [v for g in EVENTS.values() for v in g if v.endswith(".zd") and v[0] != "S"]
    slot = lambda name: turns.index(name) % 2
    set_a = make_set(NJ, ra, lambda w, j, r: pa.at[w, j, r], lambda j, w: ca.at[j, w],
                     lambda j: xa.at[j] if XA[j] else xa.at[j, 0 : ra // 4], lambda j, w: ya.at[j, 0] if w == 0 else xa.at[j, ra // 4 :], lambda j, k: za.at[j, k], lambda j, b: ga.at[slot(f"A{j}.zd"), b], XA)
    rb, b4 = pb.shape[1], pb.shape[1] // 4
    oth_b = lambda j, r: pa.at[1, j % 2, r, pl.ds(al(j // 2 * WB, WB), WB)]

    def buf_b(w, j, r):
        return oth_b(j, r) if w else pb.at[j, r]

    set_b = make_set(NJ, rb, buf_b, lambda j, w: ca.at[j, w, 0 : 2 * b4, lanes],
                     lambda j: xb.at[j] if XB[j] else xb.at[j, 0:b4], lambda j, w: yb.at[j, 0] if w == 0 else xb.at[j, b4:],
                     lambda j, k: zb.at[j, k],
                     lambda j, b: ga.at[slot(f"B{j}.zd"), b, 0 : zb.shape[2], lanes], XB)
    set_p = make_set(1, rb, lambda w, j, r: op.at[r] if w else pp.at[r], lambda j, w: cp.at[w],
                     lambda j: xp.at[0] if XP[0] else xp.at[0, 0:b4], lambda j, w: yp.at[0, 0] if w == 0 else xp.at[0, b4:],
                     lambda j, k: zp_.at[0, k],
                     lambda j, b: ga.at[slot("P.zd"), b, 0 : zb.shape[2], lanes], XP)
    set_s = make_set(1, ps.shape[2], lambda w, j, r: ps.at[w, j, r], lambda j, w: cs.at[j, w],
                     lambda j: xs.at[j], lambda j, w: ys.at[j, w], lambda j, k: zs.at[j, k], lambda j, b: gs.at[0, b], (False,))

    def out_a(j):
        own = pa.at[0, j]
        res = [(own.at[b * D : (b + 1) * D], gf.at[:, j * CH + b * WA : j * CH + (b + 1) * WA]) for b in range(CH // WA)]
        base = CH // WA * D
        res += [(own.at[base + b * CH : base + (b + 1) * CH], go.at[j * CH : (j + 1) * CH, b * WA : (b + 1) * WA])
                for b in range(D // WA)]
        return [pltpu.make_async_copy(u, v, ls.at[8 + j * 5 + i]) for i, (u, v) in enumerate(res)]

    def out_b(j):
        own = pb.at[j]
        res = [(own.at[t * D : (t + 1) * D], gq.at[t, :, j * WB : (j + 1) * WB]) for t in range(3)]
        return [pltpu.make_async_copy(u, v, ls.at[23 + j * 9 + i]) for i, (u, v) in enumerate(res)]

    def out_p(j):
        return [pltpu.make_async_copy(pp.at[b * HW : (b + 1) * HW], gp.at[:, b * WB : (b + 1) * WB], ls.at[56 + b]) for b in range(D // WB)]

    def step(name):
        def run():
            where, stage = name.split(".")
            j = int(where[1:] or 0)
            {"A": set_a, "B": set_b, "S": set_s, "P": set_p}[where[0]][stage](j)
            if stage == "cad":
                for c in {"A": out_a, "B": out_b, "S": out_s, "P": out_p}[where[0]](j):
                    c.start()
        return run

    def out_s(j):
        return [pltpu.make_async_copy(ps.at[0, 0], sm, ls.at[54])]

    def do(names):
        for name in names:
            kind, _, rest = name.partition(".")
            if kind[0] == "W":
                wstep(int(kind[1:]), int(rest[1:]))
            elif kind[:3] == "out":
                out_copy[int(kind[3:])].start()
            elif kind[:3] == "gin":
                gin_copy[int(kind[3:])].start()
            else:
                step(name)()

    def ticks(where, t):
        for g, name in enumerate(where):
            if EVENTS.get(name):
                @pl.when(t == g)
                def _(name=name):
                    do(EVENTS[name])

    def put(i, v):
        for w in (0, 1):
            for b in range(D // 128):
                ps[w, 0, i * 8 + b : i * 8 + b + 1, :] = v[:, b * 128 : (b + 1) * 128]

    ps[...] = jnp.zeros_like(ps)

    wstep(0, 0)
    wstep(0, 1)
    def ln_row(r, _):
        rr = rows_of(r)
        n1, _inv = norm(xf[rr, :].astype(F))
        a = (n1 * g1[...] + s1[...]).astype(B)
        a2[rr, :] = a
        a1t[:, rr] = a.T
        return 0

    local[0].wait()
    own_rows = ti * (T // RT // 2)
    lax.fori_loop(own_rows, own_rows + T // RT // 2, ln_row, 0)
    wstep(0, 2)
    x_copy.wait()
    bf_copy.start()
    for g in AFTER:
        if g:
            wsend(g, 0)
        else:
            c_copy.start()

    lax.fori_loop(T // RT // 2 - own_rows, T // RT - own_rows, ln_row, 0)
    bq_copy.wait()
    for c in local[3:]:
        c.wait()
    wstep(0, 3)
    do(EVENTS["ln"])

    def qkv_row(r, _):
        rr = rows_of(r)
        a = a2[rr, :]
        for t in range(3):
            v = nn(a, wqkv[:, t * D : (t + 1) * D])
            for k, b in enumerate((bq, bqo)):
                u = v[:, k * HW : (k + 1) * HW]
                if t != 1:
                    u = u + b[t // 2 : t // 2 + 1, :]
                if t == 0:
                    u = u * 0.125
                qkv[rr, t * D + k * HW : t * D + (k + 1) * HW] = u.astype(B)
        ticks(["q0", "q1", "q2", "q3"], r)
        return 0

    lax.fori_loop(0, T // RT, qkv_row, 0)

    def fwd(hp, _):
        pair_attention(hp, n, qkv, o, lse)
        ticks([f"f{i}" for i in range(6)], hp)
        return 0

    lax.fori_loop(0, NP, fwd, 0)
    local[1].wait()
    local[2].wait()
    do(EVENTS["mid0"])
    bf_copy.wait()

    def fetch(which, j):
        cols = pl.ds(al(j * CH, CH), CH)
        s1 = (wf if which == 0 else lf).at[:, cols]
        s2 = (wo if which == 0 else lo).at[cols, :]
        return [pltpu.make_async_copy(s1, wb1.at[which], ls.at[50 + which]),
                pltpu.make_async_copy(s2, wb2.at[which], ls.at[52 + which])]

    phase_mid(xf, o, wproj, bproj, g2, s2, r1, a2)
    m[...] = jnp.zeros_like(m)
    da2[...] = jnp.zeros_like(da2)
    do(EVENTS["mid1"])
    c_copy.wait()
    put(5, phase_cot(n, cf, dm))
    do(EVENTS["mid2"])
    for c in fetch(1, 0):
        c.start()

    def chunk(t, _):
        which = 1 - lax.rem(t, 2)
        j = t // 2
        for w in (0, 1):
            @pl.when(which == w)
            def _(w=w):
                for c in fetch(w, j):
                    c.wait()

        bias = jnp.where(which == 0, bfm[pl.ds(j, 1), :], bfo[pl.ds(j, 1), :])
        tot = mlp_rows(wb1.at[which], wb2.at[which], bias, a2, dm, m, da2, hd)
        for b in range(CH // 128):
            ps[which, 0, pl.ds(64 + j * 4 + b, 1), :] = tot[:, b * 128 : (b + 1) * 128]
        ticks([f"m{i}a" for i in range(6)], t)
        for w in (0, 1):
            @pl.when((which == 1 - w) & (t < 5))
            def _(w=w):
                for c in fetch(w, (t + 1) // 2):
                    c.start()
        mlp_grads(a2, dm, hd, pa.at[which, j])
        ticks([f"m{i}b" for i in range(6)], t)
        return 0

    lax.fori_loop(0, 6, chunk, 0)

    phase_back(n, cf, r1, m, da2, bout, g2, wproj, dm, hd, a2, put)
    out_own = pltpu.make_async_copy(a2.at[half(ti)], out.at[ti], ls.at[6])
    gin_own = pltpu.make_async_copy(dm.at[half(ti)], gin.at[ti], ls.at[7])
    out_own.start()
    do(EVENTS["back"])
    for w, piece in ((1, op), (0, pp)):
        g = tn(o[:, w * HW : (w + 1) * HW], dm[...]).astype(B)
        for b in range(D // WB):
            piece[b * HW : (b + 1) * HW, :] = g[:, b * WB : (b + 1) * WB]
    do(EVENTS["proj"])

    def bwd(t, _):
        which, j = (1 - t // NJ, lax.rem(t, NJ)) if ORDER == "oth" else (1 - lax.rem(t, 2), t // 2)
        hp = which * NJ + j
        pair_backward(hp, n, qkv, hd, o, lse, m)
        ticks([f"b{i}a" for i in range(6)], t)
        off = al(hp * 128, 128)
        d = jnp.concatenate([qkv[:, pl.ds(k * D + off, 128)] for k in range(3)], axis=1)
        g = nn(a1t[...], d).astype(B)

        def store(piece):
            for k in range(3):
                piece[k * D : (k + 1) * D, :] = g[:, k * 128 : (k + 1) * 128]

        @pl.when(which == 0)
        def _():
            store(pb.at[j])

        @pl.when(which == 1)
        def _():
            store(oth_b(j, slice(0, rb)))

        for k, base in ((0, 48), (2, 56)):
            v = jnp.sum(qkv[:, pl.ds(k * D + off, 128)].astype(F), axis=0, keepdims=True)
            ps[which, 0, pl.ds(base + j, 1), :] = v
        ticks([f"b{i}b" for i in range(6)], t)
        return 0

    lax.fori_loop(0, 6, bwd, 0)
    first = (T // RT // 2) * (1 - ti)
    sums = phase_end(xf, qkv, wqkv, g1, da2, dm, first, None)
    do(EVENTS["end1"])
    do(EVENTS["end1b"])
    a, b = phase_end(xf, qkv, wqkv, g1, da2, dm, T // RT // 2 - first, sums)
    put(0, a)
    put(1, b)
    gin_own.start()
    do(EVENTS["end2"])
    do(EVENTS["drain"])
    for j in range(NJ):
        for c in out_a(j) + out_b(j):
            c.wait()
    for c in out_s(0) + out_p(0) + [out_own, gin_own] + out_copy + gin_copy:
        c.wait()
    assert count[0] <= SEMS(dp)


def SEMS(dp):
    return 64 + 8 * (25 + depth(dp))


def local_call(dp, *args):
    V = pl.BlockSpec(memory_space=pltpu.VMEM)
    S = pl.BlockSpec(memory_space=pltpu.SMEM)
    A = pl.BlockSpec(memory_space=pl.ANY)
    sd = jax.ShapeDtypeStruct
    ra, rb, rsm, nz = 4 * D, 3 * D, 256, 4
    nb = max(depth(dp), 1)
    outs = (sd((2, T // 2, D), B), sd((2, T // 2, D), B), sd((3, D, HW), B), sd((HW, D), B), sd((D, FH), B),
            sd((FH, D), B), sd((rsm, 128), F), sd((D, FH), B), sd((FH, D), B))
    vm = pltpu.VMEM
    sem = pltpu.SemaphoreType.DMA

    def buffers(k, r, w, x_first, dt):
        return [vm((2, k, r, w), dt), vm((k, 2, r // 2, w), dt), vm((k, r // 2 if x_first else r // 4, w), dt),
                vm((k, 1 if x_first else 2, r // 4, w), dt), vm((k, nz, r // 4 // nz, w), dt), vm((min(k, 2), nb, r // 4 // nz, w) if dp > 16 else (1, 1, 16, 128), dt)]

    return pl.pallas_call(
        functools.partial(kernel, dp),
        out_shape=outs,
        in_specs=[S, A, A, A, V, A, A, A] + [V] * 7,
        out_specs=(A,) * 9,
        scratch_shapes=[
            vm((T, D), B), vm((T, D), B), vm((D, T), B), vm((D, 3 * D), B), vm((D, D), B), vm((2, HW), F), vm((8, CH), F), vm((8, CH), F),
            vm((2, D, CH), B), vm((2, CH, D), B), vm((T, 3 * D), B), vm((T, D), B), vm((16, T), F), vm((T, D), F),
            vm((T, D), B), vm((T, D), B), vm((T, D), F), vm((T, D), F), vm((T, 2 * CH), B),
        ] + buffers(NJ, ra, WA, True, B) + [vm((NJ, rb, WB), B)] + buffers(NJ, rb, WB, True, B)[2:5]
        + [vm((rb, WB), B), vm((rb, WB), B), vm((2, rb // 2, WB), B)] + buffers(1, rb, WB, True, B)[2:5] + buffers(1, rsm, 128, False, F)
        + [sem((SEMS(dp),)), sem((SEMS(dp),)), sem((64,)), pltpu.SemaphoreType.REGULAR((24,))],
        compiler_params=pltpu.CompilerParams(vmem_limit_bytes=VLIMIT, collective_id=0, has_side_effects=True),
    )(*args)


VLIMIT = 63 * 2**20 + 2**19


def body(dp, inputs, cotangent, lengths, gain_one, shift_one, qkv_weight, qv_bias, proj_weight, proj_bias, gain_two,
         shift_two, fc_weight, fc_bias, out_weight, out_bias):
    res = local_call(
        dp, lengths.reshape(1, 2), inputs.reshape(2, T // 2, D), cotangent.reshape(2, T // 2, D),
        jnp.transpose(qkv_weight, (1, 0, 2)), qv_bias, proj_weight, fc_weight, out_weight, gain_one, shift_one,
        proj_bias, gain_two, shift_two, out_bias, fc_bias)
    out, gin, gq, gp, gf, go, gqv, gfb, *vec = widen(*res[:7])
    rows = lambda v: v[:, None]
    return (rows(out), rows(gin), vec[0], vec[1], jnp.transpose(gq, (1, 0, 2)), gqv, gp, vec[2], vec[3], vec[4], gf, gfb,
            go, vec[5])


def widen_kernel(*refs):
    srcs, sm, dsts, (gqv, gfb, *vec), (ins, outs, si, so) = refs[:6], refs[6], refs[7:13], refs[13:21], refs[21:]
    tiles = []
    for s, d in zip(srcs, dsts):
        for a in range(s.shape[0] if len(s.shape) == 3 else 1):
            u, v = (s.at[a], d.at[a]) if len(s.shape) == 3 else (s, d)
            step = min(512, u.shape[0])
            for b in range(0, u.shape[0], step):
                tiles.append((u.at[b : b + step], v.at[b : b + step], u.shape[1], min(step, u.shape[0] - b)))
    place, row, col = [], 0, 0
    for _u, _v, wide, n in tiles:
        if col + wide > FH:
            row, col = row + 1, 0
        place.append((row, pl.ds(0, n), pl.ds(col, wide)))
        col += wide
    def load(i):
        r, a, b = place[i]
        return pltpu.make_async_copy(tiles[i][0], ins.at[r, a, b], si.at[i])
    def save(i):
        r, a, b = place[i]
        return pltpu.make_async_copy(outs.at[r, a, b], tiles[i][1], so.at[i])
    for i in range(len(tiles)):
        load(i).start()
    for i in range(6):
        for b in range(D // 128):
            vec[i][b * 128 : (b + 1) * 128] = sm[i * 8 + b, :]
    for b in range(FH // 128):
        gfb[b * 128 : (b + 1) * 128] = sm[64 + b, :]
    for b in range(HW // 128):
        gqv[0:1, b * 128 : (b + 1) * 128] = sm[48 + b : 49 + b, :]
        gqv[1:2, b * 128 : (b + 1) * 128] = sm[56 + b : 57 + b, :]
    for i in range(len(tiles)):
        load(i).wait()
        r, _a, b = place[i]
        n = tiles[i][3]

        def step(k, _):
            rr = pl.ds(pl.multiple_of(k * 64, 64), 64)
            outs[r, rr, b] = ins[r, rr, b].astype(F)
            return 0

        lax.fori_loop(0, n // 64, step, 0)
        save(i).start()
    for i in range(len(tiles)):
        save(i).wait()


def widen(*args):
    V = pl.BlockSpec(memory_space=pltpu.VMEM)
    A = pl.BlockSpec(memory_space=pl.ANY)
    sd = jax.ShapeDtypeStruct
    wide = [sd(v.shape, F) for v in args[:6]]
    small = [sd((2, HW), F), sd((FH,), F)] + [sd((D,), F)] * 6
    sem = pltpu.SemaphoreType.DMA
    return pl.pallas_call(
        widen_kernel,
        out_shape=tuple(wide + small),
        in_specs=[A] * 6 + [V],
        out_specs=tuple([A] * 6 + [V] * 8),
        scratch_shapes=[pltpu.VMEM((9, 512, FH), B), pltpu.VMEM((9, 512, FH), F), sem((24,)), sem((24,))],
        compiler_params=pltpu.CompilerParams(vmem_limit_bytes=56 * 2**20),
    )(*args)


def solution(mesh):
    dp = P(None, "dp", "tensor", None)
    return jax.shard_map(
        functools.partial(body, mesh.shape["dp"]),
        mesh=mesh,
        in_specs=(dp, dp, P(None, "dp"), P(), P(), P(None, None, "tensor"), P(None, "tensor"), P("tensor", None), P(),
                  P(), P(), P(None, "tensor"), P("tensor"), P("tensor", None), P()),
        out_specs=(dp, dp, P(), P(), P(None, None, "tensor"), P(None, "tensor"), P("tensor", None), P(), P(), P(),
                   P(None, "tensor"), P("tensor"), P("tensor", None), P()),
        check_vma=False,
    )
```

```python
import functools

import jax
import jax.numpy as jnp
from jax import lax
from jax.experimental import pallas as pl
from jax.experimental.pallas import tpu as pltpu
from jax.sharding import PartitionSpec as P

F = jnp.float32
B = jnp.bfloat16
T = 1024
D = 768
HD = 64
HW = 384
FF = 3072
FH = 1536
CH = 512
RT = 256
QB = 256
NP = 6
EPS = 1e-05
SB = 48 ** (-0.5)
RC = 0.7978845608028654
CC = 0.044715


def nn(a, b):
    return lax.dot_general(a, b, (((1,), (0,)), ((), ())), preferred_element_type=F)


def nt(a, b):
    return lax.dot_general(a, b, (((1,), (1,)), ((), ())), preferred_element_type=F)


def tn(a, b):
    return lax.dot_general(a, b, (((0,), (0,)), ((), ())), preferred_element_type=F)


def rows_of(r):
    return pl.ds(pl.multiple_of(r * RT, RT), RT)


def norm(v):
    cen = v - jnp.mean(v, axis=-1, keepdims=True)
    inv = lax.rsqrt(jnp.mean(cen * cen, axis=-1, keepdims=True) + EPS)
    return cen * inv, inv


def norm_back(e, n, inv):
    return inv * (e - jnp.mean(e, axis=-1, keepdims=True) - n * jnp.mean(e * n, axis=-1, keepdims=True))


def gelu_pair(u):
    u2 = u * u
    t = jnp.tanh(RC * (u + CC * u2 * u))
    hp = 0.5 * (1.0 + t)
    return u * hp, hp + (0.5 * RC) * u * (1.0 - t * t) * (1.0 + (3.0 * CC) * u2)


def pair_attention(hp, n, qkv, o, lse):
    off = pl.multiple_of(hp * 128, 128)
    lane = lax.broadcasted_iota(jnp.int32, (QB, 128), 1)
    for qb in range(T // QB):
        ext = (qb + 1) * QB
        q2 = qkv[pl.ds(qb * QB, QB), pl.ds(off, 128)]
        k2 = qkv[pl.ds(0, ext), pl.ds(D + off, 128)]
        v2 = qkv[pl.ds(0, ext), pl.ds(2 * D + off, 128)]
        key = lax.broadcasted_iota(jnp.int32, (ext, QB), 0)
        qi = lax.broadcasted_iota(jnp.int32, (ext, QB), 1) + qb * QB
        bound = jnp.minimum(qi + 1, n)
        outs = []
        for h in range(2):
            qm = jnp.where((lane // HD) == h, q2, jnp.zeros_like(q2))
            s = jnp.where(key < bound, nt(k2, qm), -1e30)
            m = jnp.max(s, axis=0, keepdims=True)
            e = jnp.exp(s - m)
            l = jnp.sum(e, axis=0, keepdims=True)
            pb = (e * (1.0 / l)).astype(B)
            outs.append(tn(pb, v2))
            lse[pl.ds(hp * 2 + h, 1), pl.ds(qb * QB, QB)] = m + jnp.log(l)
        o[pl.ds(qb * QB, QB), pl.ds(off, 128)] = jnp.where(lane < HD, outs[0], outs[1]).astype(B)


def pair_backward(hp, n, qkv, do, o, lse, acc):
    off = pl.multiple_of(hp * 128, 128)
    lane = lax.broadcasted_iota(jnp.int32, (QB, 128), 1)
    for qb in reversed(range(T // QB)):
        ext = (qb + 1) * QB
        rq = pl.ds(qb * QB, QB)
        q2 = qkv[rq, pl.ds(off, 128)]
        k2 = qkv[pl.ds(0, ext), pl.ds(D + off, 128)]
        v2 = qkv[pl.ds(0, ext), pl.ds(2 * D + off, 128)]
        do2 = do[rq, pl.ds(off, 128)]
        o2 = o[rq, pl.ds(off, 128)]
        prod = (do2.astype(F) * o2.astype(F)).T
        key = lax.broadcasted_iota(jnp.int32, (ext, QB), 0)
        qi = lax.broadcasted_iota(jnp.int32, (ext, QB), 1) + qb * QB
        bound = jnp.minimum(qi + 1, n)
        dqs, dks, dvs = [], [], []
        for h in range(2):
            hm = (lane // HD) == h
            qm = jnp.where(hm, q2, jnp.zeros_like(q2))
            dm = jnp.where(hm, do2, jnp.zeros_like(do2))
            dd = jnp.sum(prod[h * HD : (h + 1) * HD], axis=0, keepdims=True)
            ls = lse[pl.ds(hp * 2 + h, 1), rq]
            p = jnp.where(key < bound, jnp.exp(nt(k2, qm) - ls), 0.0)
            ds = (p * (nt(v2, dm) - dd)).astype(B)
            dqs.append(tn(k2, ds).T)
            dks.append(nn(ds, qm))
            dvs.append(nn(p.astype(B), dm))
        qkv[rq, pl.ds(off, 128)] = (jnp.where(lane < HD, dqs[0], dqs[1]) * 0.125).astype(B)
        dk = dks[0] + dks[1]
        dv = dvs[0] + dvs[1]
        if qb == T // QB - 1:
            acc[:, 0:128] = dk
            acc[:, 128:256] = dv
        else:
            acc[pl.ds(0, ext), 0:128] += dk
            acc[pl.ds(0, ext), 128:256] += dv
    qkv[:, pl.ds(D + off, 128)] = acc[:, 0:128].astype(B)
    qkv[:, pl.ds(2 * D + off, 128)] = acc[:, 128:256].astype(B)


def phase_mid(x, o, wproj, bproj, g2, s2, r1, a2):
    def row(r, _):
        rr = rows_of(r)
        v = x[rr, :].astype(F) + SB * (nn(o[rr, :], wproj[...]) + bproj[...])
        r1[rr, :] = v
        n2, _inv = norm(v)
        a2[rr, :] = (n2 * g2[...] + s2[...]).astype(B)
        return 0

    lax.fori_loop(0, T // RT, row, 0)


def phase_cot(n, c, dm):
    def row(r, ob):
        rr = rows_of(r)
        ids = lax.broadcasted_iota(jnp.int32, (RT, 1), 0) + r * RT
        cs = SB * (c[rr, :].astype(F) * (ids < n).astype(F))
        dm[rr, :] = cs.astype(B)
        return ob + jnp.sum(cs, axis=0, keepdims=True)

    return lax.fori_loop(0, T // RT, row, jnp.zeros((1, D), F))


def phase_back(n, c, r1, m, da2, bout, g2, wproj, dattn, do, out, put):
    def row(r, acc):
        rr = rows_of(r)
        v = r1[rr, :]
        out[rr, :] = (v + SB * (m[rr, :] + bout[...])).astype(B)
        n2, inv = norm(v)
        g = da2[rr, :]
        ids = lax.broadcasted_iota(jnp.int32, (RT, 1), 0) + r * RT
        dr = c[rr, :].astype(F) * (ids < n).astype(F) + norm_back(g * g2[...], n2, inv)
        da2[rr, :] = dr
        sr = SB * dr
        sb = sr.astype(B)
        dattn[rr, :] = sb
        do[rr, 0:D] = nt(sb, wproj[...]).astype(B)
        total = lambda w: jnp.sum(w, axis=0, keepdims=True)
        return acc[0] + total(g * n2), acc[1] + total(g), acc[2] + total(sr)

    z = jnp.zeros((1, D), F)
    a, b, p = lax.fori_loop(0, T // RT, row, (z, z, z))
    put(2, p)
    put(3, a)
    put(4, b)


def phase_end(x, qkv, wqkv, g1, dr1, gin, first, sums):
    def row(r, acc):
        rr = rows_of(r)
        g = nt(qkv[rr, :], wqkv[...])
        n1, inv = norm(x[rr, :].astype(F))
        gin[rr, :] = (dr1[rr, :] + norm_back(g * g1[...], n1, inv)).astype(B)
        total = lambda w: jnp.sum(w, axis=0, keepdims=True)
        return acc[0] + total(g * n1), acc[1] + total(g)

    z = jnp.zeros((1, D), F)
    return lax.fori_loop(first, first + T // RT // 2, row, (z, z) if sums is None else sums)


EVENTS = {
    "ln": (),
    "q0": (),
    "q1": (),
    "q2": (),
    "q3": ("W1.w0",),
    "f0": ("W4.w0",),
    "f1": ("W2.w0", "W1.w1",),
    "f2": ("W3.w0", "W4.w1",),
    "f3": ("W2.w1",),
    "f4": ("W4.w2",),
    "f5": ("W1.w2", "W4.w3",),
    "mid0": (),
    "mid1": ("W2.w2",),
    "mid2": ("W1.w3",),
    "m0a": ("W3.w1", "W2.w3",),
    "m0b": ("A0.cs1",),
    "m1a": (),
    "m1b": ("A0.cs0", "A0.cd1",),
    "m2a": ("W3.w2",),
    "m2b": ("A1.cs1", "A0.cd0",),
    "m3a": ("W3.w3", "A0.yd1",),
    "m3b": ("A1.cs0", "A1.cd1",),
    "m4a": ("A1.cd0", "A0.yd0",),
    "m4b": ("A2.cs1", "A0.xd",),
    "m5a": (),
    "m5b": ("A2.cs0", "A2.cd1", "A1.yd1",),
    "back": ("A2.cd0", "A0.zd",),
    "proj": ("P.cs1", "P.cs0",),
    "b0a": ("out0", "A1.yd0", "A1.xd", "P.cd1", "P.cd0",),
    "b0b": ("B0.cs1",),
    "b1a": ("A2.yd1", "A0.zad",),
    "b1b": ("B1.cs1",),
    "b2a": ("A2.yd0", "A1.zd", "B0.cd1", "P.xd", "B1.cd1",),
    "b2b": ("B2.cs1",),
    "b3a": ("B2.cd1",),
    "b3b": ("B0.cs0", "A2.xd", "A0.yad",),
    "b4a": ("B0.cd0", "P.yd0", "A1.zad",),
    "b4b": ("B1.cs0", "A0.cad",),
    "b5a": ("A2.zd", "B1.cd0", "B0.xd", "B1.xd",),
    "b5b": ("B2.cs0", "A1.yad", "out1", "B2.cd0", "P.zd",),
    "end1": ("B2.xd", "out2", "B0.yd0",),
    "end1b": (),
    "end2": ("S.cs1", "S.cs0", "A1.cad", "B1.yd0",),
    "drain": ("A2.zad", "out3", "S.cd1", "P.zad", "B2.yd0", "S.cd0", "B0.zd", "gin0", "B1.zd", "gin1", "A2.yad",
        "S.yd1", "B2.zd", "P.yad", "gin2", "B0.zad", "S.yd0", "A2.cad", "S.xd", "B1.zad", "P.cad", "gin3",
        "B0.yad", "B2.zad", "S.zd", "B1.yad", "B0.cad", "S.zad", "B2.yad", "B1.cad", "S.yad", "B2.cad", "S.cad",),
}
WAY = ("zy", "zy", "yz", "yz", "yz")
XA = (False, False, False)
XB = (True, True, True)
XP = (True,)
FIRST = "oth"
AFTER = (1, 4, 2, 3, 0)
COUNT = 4
ORDER = "oth"
MESH = pl.DeviceIdType.MESH
NJ = 3
WA = 256
WB = 128


def each(n, fn):
    if n <= 3:
        for d in range(1, n + 1):
            fn(d)
    else:
        lax.fori_loop(1, n + 1, lambda d, _: (fn(d), 0)[1], 0)


def add_rows(rows, dst, srcs):
    step = next(s for s in (192, 128, 64, 32, 16) if rows % s == 0)

    def tile(i, _):
        rr = pl.ds(pl.multiple_of(i * step, step), step)
        v = dst[rr, :].astype(F)
        for s in srcs:
            v = v + s[rr, :].astype(F)
        dst[rr, :] = v.astype(dst.dtype)
        return 0

    lax.fori_loop(0, rows // step, tile, 0)


def depth(dp):
    return (dp // 16 - 1).bit_length()


def mlp_rows(w1, w2, bias, a2, dm, m, da2, hd):
    tot = jnp.zeros((1, CH), F)
    for r in range(T // RT):
        rr = pl.ds(r * RT, RT)
        u = nn(a2[rr, :], w1[...]) + bias
        h, sl = gelu_pair(u)
        hb = h.astype(B)
        hd[rr, 0:CH] = hb
        du = (nt(dm[rr, :], w2[...]) * sl).astype(B)
        hd[rr, CH : 2 * CH] = du
        m[rr, :] += nn(hb, w2[...])
        da2[rr, :] += nt(du, w1[...])
        tot = tot + jnp.sum(du.astype(F), axis=0, keepdims=True)
    return tot


def mlp_grads(a2, dm, hd, piece):
    for k in range(D // 256):
        g = tn(a2[:, k * 256 : (k + 1) * 256], hd[:, CH : 2 * CH]).astype(B)
        for b in range(CH // WA):
            piece[b * D + k * 256 : b * D + (k + 1) * 256, :] = g[:, b * WA : (b + 1) * WA]
    base = CH // WA * D
    for k in range(CH // 256):
        g = tn(hd[:, k * 256 : (k + 1) * 256], dm[...]).astype(B)
        for b in range(D // WA):
            piece[base + b * CH + k * 256 : base + b * CH + (k + 1) * 256, :] = g[:, b * WA : (b + 1) * WA]


class Row:
    def __init__(self, ref):
        self.ref = ref

    def __getitem__(self, _):
        return self.ref[...].reshape(1, -1)


def kernel(dp, lens, inp, cot, wq, bq, wp, wf, wo, g1, s1, bproj, g2, s2, bout, fcb,
           out, gin, gq, gp, gf, go, sm, lf, lo,
           xf, cf, a1t, wqkv, wproj, bqo, bfm, bfo, wb1, wb2, qkv, o, lse, r1, a2, dm, m, da2, hd,
           pa, ca, xa, ya, za, ga, pb, xb, yb, zb, pp, op, cp, xp, yp, zp_, ps, cs, xs, ys, zs, gs, ss, rs, ls, ready):
    g1, s1, bproj, g2, s2, bout = (Row(v) for v in (g1, s1, bproj, g2, s2, bout))
    ti = lax.axis_index("tensor")
    me = lax.axis_index("dp")
    nz = 4
    cc = lax.rem(me, 2)
    yy = lax.rem(me // 2, 2)
    zi = lax.rem(me // 4, nz)
    beyond = [{"dp": me + (1 - 2 * lax.rem(me // (16 << b), 2)) * (16 << b)} for b in range(depth(dp))]
    z1 = lax.rem(zi, 2)
    X = {"tensor": 1 - ti}
    C = {"dp": me + 1 - 2 * cc}
    Y = {"dp": me + 2 - 4 * yy}
    Z1 = {"dp": me + 4 - 8 * z1}
    zp = lambda k: {"dp": me + (k - zi) * 4}
    al = pl.multiple_of
    count = [0]
    flags = [0]

    def new(k=1):
        count[0] += k
        return count[0] - k

    def rc(src, dst, i, dev, j=None):
        return pltpu.make_async_remote_copy(src_ref=src, dst_ref=dst, send_sem=ss.at[i], recv_sem=rs.at[i if j is None else j],
                                            device_id=dev, device_id_type=MESH)

    bar = pltpu.get_barrier_semaphore()
    for dev in (X, C, Y):
        pl.semaphore_signal(bar, inc=1, device_id=dev, device_id_type=MESH)
    each(nz - 1, lambda d: pl.semaphore_signal(bar, inc=1, device_id=zp(lax.rem(zi + d, nz)), device_id_type=MESH))
    for dev in beyond:
        pl.semaphore_signal(bar, inc=1, device_id=dev, device_id_type=MESH)
    pl.semaphore_wait(bar, 3 + nz - 1 + len(beyond))

    def units(group):
        if group == 0:
            return [(wq.at[t], lambda r, t=t: wqkv.at[r, t * D + HW : (t + 1) * D], D) for t in range(3)]
        if group == 4:
            return [(wp, lambda r: wproj.at[pl.ds(al(HW + r.start, 16), r.size), :], HW)]
        j = group - 1
        cols = slice(j * CH, (j + 1) * CH)
        return [(wf.at[:, cols], lambda r: lf.at[r, cols], D),
                (wo.at[cols, :], lambda r: lo.at[pl.ds(al(j * CH + r.start, 16), r.size), :], CH)]

    wsem = [new(4 * len(units(g))) for g in range(5)]

    def wcopies(group, stage):
        res = []
        first, second = ((z1, Z1), (yy, Y))[:: 1 if WAY[group] == "zy" else -1]
        for i, (own, land, n) in enumerate(units(group)):
            e = n // 8
            if stage < 2:
                r = pl.ds(al((cc * 4 + second[0] * 2 + first[0]) * e, 16), e)
            elif stage == 2:
                r = pl.ds(al((cc * 2 + second[0]) * 2 * e, 16), 2 * e)
            else:
                r = pl.ds(al(cc * 4 * e, 16), 4 * e)
            src = own.at[r, :] if stage == 0 else land(r)
            dev = (X, first[1], second[1], C)[stage]
            res.append(rc(src, land(r), wsem[group] + stage * len(units(group)) + i, dev))
        return res

    def wsend(group, stage):
        for c in wcopies(group, stage):
            c.start()

    def wstep(group, stage):
        nexts = wcopies(group, stage + 1) if stage < 3 else [None] * len(units(group))
        for c, d in zip(wcopies(group, stage), nexts):
            c.wait()
            if d is not None:
                d.start()

    half = lambda i: pl.ds(al(i * (T // 2), T // 2), T // 2)
    si = new(12)
    x_copy = rc(inp.at[1 - ti], xf.at[half(ti)], si, X)
    c_copy = rc(cot.at[1 - ti], cf.at[half(ti)], si + 1, X)
    bq_copy = rc(bq, bqo, si + 2, X)
    bf_copy = rc(bfm, bfo, si + 3, X)
    def rows_back(v, res, i):
        q = T // 2 // COUNT
        there = lambda b, k: pl.ds(al(b * (T // 2) + k * q, 16), q)
        return [rc(v.at[there(1 - ti, k)], res.at[ti, k * q : (k + 1) * q], si + i + k, X) for k in range(COUNT)]

    out_copy = rows_back(a2, out, 4)
    gin_copy = rows_back(dm, gin, 8)
    local = [pltpu.make_async_copy(inp.at[ti], xf.at[half(ti)], ls.at[0]),
             pltpu.make_async_copy(cot.at[ti], cf.at[half(ti)], ls.at[1]),
             pltpu.make_async_copy(wp, wproj.at[0:HW], ls.at[2])]
    local += [pltpu.make_async_copy(wq.at[t], wqkv.at[:, t * D : t * D + HW], ls.at[3 + t]) for t in range(3)]
    wsend(0, 0)
    bq_copy.start()
    x_copy.start()
    for c in local:
        c.start()

    n = lens[0, ti]
    for j in range(NJ):
        bfm[j : j + 1, :] = fcb[j * CH : (j + 1) * CH].reshape(1, CH)
    bfm[NJ:, :] = jnp.zeros((8 - NJ, CH), F)

    def make_set(k_pieces, rows, buf, co, xr, yr, zr, gr, xs_first):
        h, q = rows // 2, rows // 4
        s = q // nz
        base = [new(9 + 4 * nz + len(beyond)) for _ in range(k_pieces)]
        flag = flags[0]
        flags[0] += 3 * k_pieces
        mine = al(cc * h, 16)
        keep = al(cc * h + yy * q, 16)
        give = al(cc * h + (1 - yy) * q, 16)
        shard = lambda k: pl.ds(al(keep + k * s, 8), s)

        def swap_c(j, w):
            return rc(buf(w, j, pl.ds(al((1 - cc) * h, 16), h)), co(j, w), base[j] + w, C)

        def swap_x(j):
            src = buf(1, j, pl.ds(mine, h)) if xs_first[j] else buf(1, j, pl.ds(keep, q))
            return rc(src, xr(j), base[j] + 2, X)

        def swap_y(j, w):
            return rc(buf(w, j, pl.ds(give, q)), yr(j, w), base[j] + 3 + w, Y)

        def z_out(j):
            each(nz - 1, lambda d: z_one(j, d).start())

        def z_one(j, d):
            k = lax.rem(zi + d, nz)
            return rc(buf(0, j, shard(k)), zr(j, zi), base[j] + 9 + k, zp(k), base[j] + 9 + nz + zi)

        def z_in(j):
            def one(d):
                z_one(j, d).wait_send()
                k = lax.rem(zi + d, nz)
                rc(zr(j, k), zr(j, k), base[j] + 9 + k, zp(k), base[j] + 9 + nz + k).wait_recv()

            each(nz - 1, one)

        def za_one(j, d):
            k = lax.rem(zi + d, nz)
            return rc(buf(0, j, shard(zi)), buf(0, j, shard(zi)), base[j] + 9 + 2 * nz + k, zp(k), base[j] + 9 + 3 * nz + zi)

        def za_in(j):
            def one(d):
                za_one(j, d).wait_send()
                k = lax.rem(zi + d, nz)
                rc(buf(0, j, shard(k)), buf(0, j, shard(k)), base[j] + 9 + 2 * nz + k, zp(k), base[j] + 9 + 3 * nz + k).wait_recv()

            each(nz - 1, one)

        def all_y(j):
            r = pl.ds(keep, q)
            return rc(buf(0, j, r), buf(0, j, r), base[j] + 5, Y)

        def all_c(j):
            r = pl.ds(mine, h)
            return rc(buf(0, j, r), buf(0, j, r), base[j] + 6, C)

        def free(j, i, dev):
            pl.semaphore_signal(ready.at[flag + 3 * j + i], inc=1, device_id=dev, device_id_type=MESH)

        def freed(j, i, k):
            pl.semaphore_wait(ready.at[flag + 3 * j + i], k)

        def cs(j, w):
            swap_c(j, w).start()

        def cd(j, w):
            swap_c(j, w).wait()
            if w == 0:
                free(j, 0, C)
            add_rows(h, buf(w, j, pl.ds(mine, h)), [co(j, w)])
            if not xs_first[j]:
                swap_y(j, w).start()
            elif w == 1:
                swap_x(j).start()

        def yd(j, w):
            swap_y(j, w).wait()
            if w == 0:
                free(j, 1, Y)
            add_rows(q, buf(w, j, pl.ds(keep, q)), [yr(j, w)])
            if xs_first[j]:
                z_out(j)
            elif w == 1:
                swap_x(j).start()

        def xd(j):
            swap_x(j).wait()
            if xs_first[j]:
                add_rows(h, buf(0, j, pl.ds(mine, h)), [xr(j)])
                swap_y(j, 0).start()
            else:
                add_rows(q, buf(0, j, pl.ds(keep, q)), [xr(j)])
                z_out(j)

        def zd(j):
            z_in(j)
            each(nz - 1, lambda d: free(j, 2, zp(lax.rem(zi + d, nz))))
            add_rows(s, buf(0, j, shard(zi)), [zr(j, lax.rem(zi + d, nz)) for d in range(1, nz)])
            for b, dev in enumerate(beyond):
                copy = rc(buf(0, j, shard(zi)), gr(j, b), base[j] + 9 + 4 * nz + b, dev)
                copy.start()
                copy.wait()
                add_rows(s, buf(0, j, shard(zi)), [gr(j, b)])
            freed(j, 2, nz - 1)
            each(nz - 1, lambda d: za_one(j, d).start())

        def zad(j):
            za_in(j)
            freed(j, 1, 1)
            all_y(j).start()

        def yad(j):
            all_y(j).wait()
            freed(j, 0, 1)
            all_c(j).start()

        def cad(j):
            all_c(j).wait()

        return dict(cs1=lambda j: cs(j, 1), cs0=lambda j: cs(j, 0), cd1=lambda j: cd(j, 1), cd0=lambda j: cd(j, 0),
                    yd1=lambda j: yd(j, 1), yd0=lambda j: yd(j, 0), xd=xd, zd=zd, zad=zad, yad=yad, cad=cad)

    ra = pa.shape[2]
    lanes = slice(0, WB)
    turns = [v for g in EVENTS.values() for v in g if v.endswith(".zd") and v[0] != "S"]
    slot = lambda name: turns.index(name) % 2
    set_a = make_set(NJ, ra, lambda w, j, r: pa.at[w, j, r], lambda j, w: ca.at[j, w],
                     lambda j: xa.at[j] if XA[j] else xa.at[j, 0 : ra // 4], lambda j, w: ya.at[j, 0] if w == 0 else xa.at[j, ra // 4 :], lambda j, k: za.at[j, k], lambda j, b: ga.at[slot(f"A{j}.zd"), b], XA)
    rb, b4 = pb.shape[1], pb.shape[1] // 4
    oth_b = lambda j, r: pa.at[1, j % 2, r, pl.ds(al(j // 2 * WB, WB), WB)]

    def buf_b(w, j, r):
        return oth_b(j, r) if w else pb.at[j, r]

    set_b = make_set(NJ, rb, buf_b, lambda j, w: ca.at[j, w, 0 : 2 * b4, lanes],
                     lambda j: xb.at[j] if XB[j] else xb.at[j, 0:b4], lambda j, w: yb.at[j, 0] if w == 0 else xb.at[j, b4:],
                     lambda j, k: zb.at[j, k],
                     lambda j, b: ga.at[slot(f"B{j}.zd"), b, 0 : zb.shape[2], lanes], XB)
    set_p = make_set(1, rb, lambda w, j, r: op.at[r] if w else pp.at[r], lambda j, w: cp.at[w],
                     lambda j: xp.at[0] if XP[0] else xp.at[0, 0:b4], lambda j, w: yp.at[0, 0] if w == 0 else xp.at[0, b4:],
                     lambda j, k: zp_.at[0, k],
                     lambda j, b: ga.at[slot("P.zd"), b, 0 : zb.shape[2], lanes], XP)
    set_s = make_set(1, ps.shape[2], lambda w, j, r: ps.at[w, j, r], lambda j, w: cs.at[j, w],
                     lambda j: xs.at[j], lambda j, w: ys.at[j, w], lambda j, k: zs.at[j, k], lambda j, b: gs.at[0, b], (False,))

    def out_a(j):
        own = pa.at[0, j]
        res = [(own.at[b * D : (b + 1) * D], gf.at[:, j * CH + b * WA : j * CH + (b + 1) * WA]) for b in range(CH // WA)]
        base = CH // WA * D
        res += [(own.at[base + b * CH : base + (b + 1) * CH], go.at[j * CH : (j + 1) * CH, b * WA : (b + 1) * WA])
                for b in range(D // WA)]
        return [pltpu.make_async_copy(u, v, ls.at[8 + j * 5 + i]) for i, (u, v) in enumerate(res)]

    def out_b(j):
        own = pb.at[j]
        res = [(own.at[t * D : (t + 1) * D], gq.at[t, :, j * WB : (j + 1) * WB]) for t in range(3)]
        return [pltpu.make_async_copy(u, v, ls.at[23 + j * 9 + i]) for i, (u, v) in enumerate(res)]

    def out_p(j):
        return [pltpu.make_async_copy(pp.at[b * HW : (b + 1) * HW], gp.at[:, b * WB : (b + 1) * WB], ls.at[56 + b]) for b in range(D // WB)]

    def step(name):
        def run():
            where, stage = name.split(".")
            j = int(where[1:] or 0)
            {"A": set_a, "B": set_b, "S": set_s, "P": set_p}[where[0]][stage](j)
            if stage == "cad":
                for c in {"A": out_a, "B": out_b, "S": out_s, "P": out_p}[where[0]](j):
                    c.start()
        return run

    def out_s(j):
        return [pltpu.make_async_copy(ps.at[0, 0], sm, ls.at[54])]

    def do(names):
        for name in names:
            kind, _, rest = name.partition(".")
            if kind[0] == "W":
                wstep(int(kind[1:]), int(rest[1:]))
            elif kind[:3] == "out":
                out_copy[int(kind[3:])].start()
            elif kind[:3] == "gin":
                gin_copy[int(kind[3:])].start()
            else:
                step(name)()

    def ticks(where, t):
        for g, name in enumerate(where):
            if EVENTS.get(name):
                @pl.when(t == g)
                def _(name=name):
                    do(EVENTS[name])

    def put(i, v):
        for w in (0, 1):
            for b in range(D // 128):
                ps[w, 0, i * 8 + b : i * 8 + b + 1, :] = v[:, b * 128 : (b + 1) * 128]

    ps[...] = jnp.zeros_like(ps)

    wstep(0, 0)
    wstep(0, 1)
    def ln_row(r, _):
        rr = rows_of(r)
        n1, _inv = norm(xf[rr, :].astype(F))
        a = (n1 * g1[...] + s1[...]).astype(B)
        a2[rr, :] = a
        a1t[:, rr] = a.T
        return 0

    local[0].wait()
    own_rows = ti * (T // RT // 2)
    lax.fori_loop(own_rows, own_rows + T // RT // 2, ln_row, 0)
    wstep(0, 2)
    x_copy.wait()
    bf_copy.start()
    for g in AFTER:
        if g:
            wsend(g, 0)
        else:
            c_copy.start()

    lax.fori_loop(T // RT // 2 - own_rows, T // RT - own_rows, ln_row, 0)
    bq_copy.wait()
    for c in local[3:]:
        c.wait()
    def qkv_rows(t):
        def row(r, _):
            rr = rows_of(r)
            v = nn(a2[rr, :], wqkv[:, t * D : (t + 1) * D])
            for k, b in enumerate((bq, bqo)):
                u = v[:, k * HW : (k + 1) * HW]
                if t != 1:
                    u = u + b[t // 2 : t // 2 + 1, :]
                if t == 0:
                    u = u * 0.125
                qkv[rr, t * D + k * HW : t * D + (k + 1) * HW] = u.astype(B)
            return 0

        wcopies(0, 3)[t].wait()
        lax.fori_loop(0, T // RT, row, 0)

    for t, names in enumerate((("ln", "q0"), ("q1",), ("q2", "q3"))):
        qkv_rows(t)
        for name in names:
            do(EVENTS[name])

    def fwd(hp, _):
        pair_attention(hp, n, qkv, o, lse)
        ticks([f"f{i}" for i in range(6)], hp)
        return 0

    lax.fori_loop(0, NP, fwd, 0)
    local[1].wait()
    local[2].wait()
    do(EVENTS["mid0"])
    bf_copy.wait()

    def fetch(which, j):
        cols = pl.ds(al(j * CH, CH), CH)
        s1 = (wf if which == 0 else lf).at[:, cols]
        s2 = (wo if which == 0 else lo).at[cols, :]
        return [pltpu.make_async_copy(s1, wb1.at[which], ls.at[50 + which]),
                pltpu.make_async_copy(s2, wb2.at[which], ls.at[52 + which])]

    phase_mid(xf, o, wproj, bproj, g2, s2, r1, a2)
    m[...] = jnp.zeros_like(m)
    da2[...] = jnp.zeros_like(da2)
    do(EVENTS["mid1"])
    c_copy.wait()
    put(5, phase_cot(n, cf, dm))
    do(EVENTS["mid2"])
    for c in fetch(1, 0):
        c.start()

    def chunk(t, _):
        which = 1 - lax.rem(t, 2)
        j = t // 2
        for w in (0, 1):
            @pl.when(which == w)
            def _(w=w):
                for c in fetch(w, j):
                    c.wait()

        bias = jnp.where(which == 0, bfm[pl.ds(j, 1), :], bfo[pl.ds(j, 1), :])
        tot = mlp_rows(wb1.at[which], wb2.at[which], bias, a2, dm, m, da2, hd)
        for b in range(CH // 128):
            ps[which, 0, pl.ds(64 + j * 4 + b, 1), :] = tot[:, b * 128 : (b + 1) * 128]
        ticks([f"m{i}a" for i in range(6)], t)
        for w in (0, 1):
            @pl.when((which == 1 - w) & (t < 5))
            def _(w=w):
                for c in fetch(w, (t + 1) // 2):
                    c.start()
        mlp_grads(a2, dm, hd, pa.at[which, j])
        ticks([f"m{i}b" for i in range(6)], t)
        return 0

    lax.fori_loop(0, 6, chunk, 0)

    phase_back(n, cf, r1, m, da2, bout, g2, wproj, dm, hd, a2, put)
    out_own = pltpu.make_async_copy(a2.at[half(ti)], out.at[ti], ls.at[6])
    gin_own = pltpu.make_async_copy(dm.at[half(ti)], gin.at[ti], ls.at[7])
    out_own.start()
    do(EVENTS["back"])
    for w, piece in ((1, op), (0, pp)):
        g = tn(o[:, w * HW : (w + 1) * HW], dm[...]).astype(B)
        for b in range(D // WB):
            piece[b * HW : (b + 1) * HW, :] = g[:, b * WB : (b + 1) * WB]
    do(EVENTS["proj"])

    def bwd(t, _):
        which, j = (1 - t // NJ, lax.rem(t, NJ)) if ORDER == "oth" else (1 - lax.rem(t, 2), t // 2)
        hp = which * NJ + j
        pair_backward(hp, n, qkv, hd, o, lse, m)
        ticks([f"b{i}a" for i in range(6)], t)
        off = al(hp * 128, 128)
        d = jnp.concatenate([qkv[:, pl.ds(k * D + off, 128)] for k in range(3)], axis=1)
        g = nn(a1t[...], d).astype(B)

        def store(piece):
            for k in range(3):
                piece[k * D : (k + 1) * D, :] = g[:, k * 128 : (k + 1) * 128]

        @pl.when(which == 0)
        def _():
            store(pb.at[j])

        @pl.when(which == 1)
        def _():
            store(oth_b(j, slice(0, rb)))

        for k, base in ((0, 48), (2, 56)):
            v = jnp.sum(qkv[:, pl.ds(k * D + off, 128)].astype(F), axis=0, keepdims=True)
            ps[which, 0, pl.ds(base + j, 1), :] = v
        ticks([f"b{i}b" for i in range(6)], t)
        return 0

    lax.fori_loop(0, 6, bwd, 0)
    first = (T // RT // 2) * (1 - ti)
    sums = phase_end(xf, qkv, wqkv, g1, da2, dm, first, None)
    do(EVENTS["end1"])
    do(EVENTS["end1b"])
    a, b = phase_end(xf, qkv, wqkv, g1, da2, dm, T // RT // 2 - first, sums)
    put(0, a)
    put(1, b)
    gin_own.start()
    do(EVENTS["end2"])
    do(EVENTS["drain"])
    for j in range(NJ):
        for c in out_a(j) + out_b(j):
            c.wait()
    for c in out_s(0) + out_p(0) + [out_own, gin_own] + out_copy + gin_copy:
        c.wait()
    assert count[0] <= SEMS(dp)


def SEMS(dp):
    return 64 + 8 * (25 + depth(dp))


def local_call(dp, *args):
    V = pl.BlockSpec(memory_space=pltpu.VMEM)
    S = pl.BlockSpec(memory_space=pltpu.SMEM)
    A = pl.BlockSpec(memory_space=pl.ANY)
    sd = jax.ShapeDtypeStruct
    ra, rb, rsm, nz = 4 * D, 3 * D, 256, 4
    nb = max(depth(dp), 1)
    outs = (sd((2, T // 2, D), B), sd((2, T // 2, D), B), sd((3, D, HW), B), sd((HW, D), B), sd((D, FH), B),
            sd((FH, D), B), sd((rsm, 128), F), sd((D, FH), B), sd((FH, D), B))
    vm = pltpu.VMEM
    sem = pltpu.SemaphoreType.DMA

    def buffers(k, r, w, x_first, dt):
        return [vm((2, k, r, w), dt), vm((k, 2, r // 2, w), dt), vm((k, r // 2 if x_first else r // 4, w), dt),
                vm((k, 1 if x_first else 2, r // 4, w), dt), vm((k, nz, r // 4 // nz, w), dt), vm((min(k, 2), nb, r // 4 // nz, w) if dp > 16 else (1, 1, 16, 128), dt)]

    return pl.pallas_call(
        functools.partial(kernel, dp),
        out_shape=outs,
        in_specs=[S, A, A, A, V, A, A, A] + [V] * 7,
        out_specs=(A,) * 9,
        scratch_shapes=[
            vm((T, D), B), vm((T, D), B), vm((D, T), B), vm((D, 3 * D), B), vm((D, D), B), vm((2, HW), F), vm((8, CH), F), vm((8, CH), F),
            vm((2, D, CH), B), vm((2, CH, D), B), vm((T, 3 * D), B), vm((T, D), B), vm((16, T), F), vm((T, D), F),
            vm((T, D), B), vm((T, D), B), vm((T, D), F), vm((T, D), F), vm((T, 2 * CH), B),
        ] + buffers(NJ, ra, WA, True, B) + [vm((NJ, rb, WB), B)] + buffers(NJ, rb, WB, True, B)[2:5]
        + [vm((rb, WB), B), vm((rb, WB), B), vm((2, rb // 2, WB), B)] + buffers(1, rb, WB, True, B)[2:5] + buffers(1, rsm, 128, False, F)
        + [sem((SEMS(dp),)), sem((SEMS(dp),)), sem((64,)), pltpu.SemaphoreType.REGULAR((24,))],
        compiler_params=pltpu.CompilerParams(vmem_limit_bytes=VLIMIT, collective_id=0, has_side_effects=True),
    )(*args)


VLIMIT = 63 * 2**20 + 2**19


def body(dp, inputs, cotangent, lengths, gain_one, shift_one, qkv_weight, qv_bias, proj_weight, proj_bias, gain_two,
         shift_two, fc_weight, fc_bias, out_weight, out_bias):
    res = local_call(
        dp, lengths.reshape(1, 2), inputs.reshape(2, T // 2, D), cotangent.reshape(2, T // 2, D),
        jnp.transpose(qkv_weight, (1, 0, 2)), qv_bias, proj_weight, fc_weight, out_weight, gain_one, shift_one,
        proj_bias, gain_two, shift_two, out_bias, fc_bias)
    out, gin, gq, gp, gf, go, gqv, gfb, *vec = widen(*res[:7])
    rows = lambda v: v[:, None]
    return (rows(out), rows(gin), vec[0], vec[1], jnp.transpose(gq, (1, 0, 2)), gqv, gp, vec[2], vec[3], vec[4], gf, gfb,
            go, vec[5])


def widen_kernel(*refs):
    srcs, sm, dsts, (gqv, gfb, *vec), (ins, outs, si, so) = refs[:6], refs[6], refs[7:13], refs[13:21], refs[21:]
    tiles = []
    for s, d in zip(srcs, dsts):
        for a in range(s.shape[0] if len(s.shape) == 3 else 1):
            u, v = (s.at[a], d.at[a]) if len(s.shape) == 3 else (s, d)
            step = min(256, u.shape[0])
            for b in range(0, u.shape[0], step):
                tiles.append((u.at[b : b + step], v.at[b : b + step], u.shape[1], min(step, u.shape[0] - b)))
    place, row, col = [], 0, 0
    for _u, _v, wide, n in tiles:
        if col + wide > FH:
            row, col = row + 1, 0
        place.append((row, pl.ds(0, n), pl.ds(col, wide)))
        col += wide
    def load(i):
        r, a, b = place[i]
        return pltpu.make_async_copy(tiles[i][0], ins.at[r, a, b], si.at[i])
    def save(i):
        r, a, b = place[i]
        return pltpu.make_async_copy(outs.at[r, a, b], tiles[i][1], so.at[i])
    for i in range(len(tiles)):
        load(i).start()
    for i in range(6):
        for b in range(D // 128):
            vec[i][b * 128 : (b + 1) * 128] = sm[i * 8 + b, :]
    for b in range(FH // 128):
        gfb[b * 128 : (b + 1) * 128] = sm[64 + b, :]
    for b in range(HW // 128):
        gqv[0:1, b * 128 : (b + 1) * 128] = sm[48 + b : 49 + b, :]
        gqv[1:2, b * 128 : (b + 1) * 128] = sm[56 + b : 57 + b, :]
    for i in range(len(tiles)):
        load(i).wait()
        r, _a, b = place[i]
        n = tiles[i][3]

        def step(k, _):
            rr = pl.ds(pl.multiple_of(k * 64, 64), 64)
            outs[r, rr, b] = ins[r, rr, b].astype(F)
            return 0

        lax.fori_loop(0, n // 64, step, 0)
        save(i).start()
    for i in range(len(tiles)):
        save(i).wait()


def widen(*args):
    V = pl.BlockSpec(memory_space=pltpu.VMEM)
    A = pl.BlockSpec(memory_space=pl.ANY)
    sd = jax.ShapeDtypeStruct
    wide = [sd(v.shape, F) for v in args[:6]]
    small = [sd((2, HW), F), sd((FH,), F)] + [sd((D,), F)] * 6
    sem = pltpu.SemaphoreType.DMA
    return pl.pallas_call(
        widen_kernel,
        out_shape=tuple(wide + small),
        in_specs=[A] * 6 + [V],
        out_specs=tuple([A] * 6 + [V] * 8),
        scratch_shapes=[pltpu.VMEM((18, 256, FH), B), pltpu.VMEM((18, 256, FH), F), sem((40,)), sem((40,))],
        compiler_params=pltpu.CompilerParams(vmem_limit_bytes=56 * 2**20),
    )(*args)


def solution(mesh):
    dp = P(None, "dp", "tensor", None)
    return jax.shard_map(
        functools.partial(body, mesh.shape["dp"]),
        mesh=mesh,
        in_specs=(dp, dp, P(None, "dp"), P(), P(), P(None, None, "tensor"), P(None, "tensor"), P("tensor", None), P(),
                  P(), P(), P(None, "tensor"), P("tensor"), P("tensor", None), P()),
        out_specs=(dp, dp, P(), P(), P(None, None, "tensor"), P(None, "tensor"), P("tensor", None), P(), P(), P(),
                   P(None, "tensor"), P("tensor"), P("tensor", None), P()),
        check_vma=False,
    )
```
